512 devices in a mesh: section: 8 (over z_hi, core), pool: 64 (over x, y, z_lo).
Axes of the slice: x: 4, y: 4, z: 16 (z_hi: 4, z_lo: 4; z = z_hi * 4 + z_lo), core: 2. Of those that a mesh axis runs over, the one named last changes fastest.
Arguments:
- activations: bfloat16 [8, 64, 16, 8, 5120], P('section', 'pool'), may hold values from -6 to 6
- cotangents: bfloat16 [8, 64, 16, 8, 5120], P('section', 'pool'), may hold values from -6 to 6
- token_counts: int32 [8, 64, 16], P('section', 'pool'), may hold values from 0 to 8, as said below
- route_ahead: int32 [8, 64, 16], P('section', 'pool'), may hold values from 0 to 63, as said below
- route_back: int32 [8, 64, 16], P('section', 'pool'), may hold values from 0 to 63, as said below
- down_rows: bfloat16 [8, 64, 5120], P('section', 'pool'), may hold values from -0.078125 to 0.078125
- up_rows: bfloat16 [8, 64, 5120], P('section', 'pool'), may hold values from -0.75 to 0.75
- norm_gain: bfloat16 [8, 5120], P('section'), may hold values from 0.099609375 to 1.8984375
Outputs:
- arrived_ahead: bfloat16 [8, 64, 12, 8, 5120], P('section', 'pool')
- arrived_back: bfloat16 [8, 64, 12, 8, 5120], P('section', 'pool')
- grad_down: float32 [8, 64, 5120], P('section', 'pool')
- grad_up: float32 [8, 64, 5120], P('section', 'pool')
The draws below stay inside these ranges and needn't reach their ends.
Inputs may be any that keep to these rules, and one draw needn't show every extreme that they name: `token_counts`: A device's live micro-batches fill its first slots, at most 12 of them, with 1 to 8 tokens each, and the later slots hold 0; the first slot of every device holds 8 tokens. `route_ahead`: the live slots of one device name distinct receivers. In every section no receiver is named by more than 12 live slots of the section's pool, and one receiver by exactly 12. Entries of empty slots are arbitrary. `route_back`: the live slots of one device name distinct devices. In every section no device is named by more than 12 live slots of the section's pool, and one by exactly 12. Entries of empty slots are arbitrary.
All inputs are finite; a program needn't handle non-finite values.
Results may differ from the reference program's by a relative error of at most 0.0053.
Values may be sent and summed in bfloat16 or wider, within the bound.
A program may use at most 128 MiB of HBM per device.

```python
import jax
import jax.numpy as jnp
from jax import lax

D = 5120
SLOTS = 16
MB_TOK = 8
CAP = 12
R = 64
SECTIONS = 8
POOL = 64


def wiring(key):
    subkeys = jax.random.split(key, 5)
    offsets = jax.vmap(lambda subkey: jax.random.permutation(subkey, POOL)[:SLOTS])(jax.random.split(subkeys[0], SECTIONS)).astype(jnp.int32)
    hot_index = jax.random.randint(subkeys[1], (SECTIONS,), 0, POOL).astype(jnp.int32)
    senders = jnp.arange(POOL, dtype=jnp.int32)
    sources = (hot_index[:, None] - offsets[:, :CAP]) % POOL
    full_rows = jnp.any(senders[None, :, None] == sources[:, None, :], axis=2)
    least_live = max(SLOTS // 2, 1)
    live_count = jax.random.randint(subkeys[2], (SECTIONS, POOL), least_live, CAP + 1).astype(jnp.int32)
    live_count = jnp.where(full_rows, CAP, live_count)
    forward_perm = jax.vmap(lambda subkey: jax.random.permutation(subkey, POOL))(jax.random.split(subkeys[3], SECTIONS)).astype(jnp.int32)
    backward_perm = jax.vmap(lambda subkey: jax.random.permutation(subkey, POOL))(jax.random.split(subkeys[4], SECTIONS)).astype(jnp.int32)
    offset_peer = (senders[None, :, None] + offsets[:, None, :]) % POOL
    return (live_count, forward_perm, backward_perm, offset_peer)


def draw_token_counts(key, part):
    live_count, forward_perm, backward_perm, offset_peer = wiring(key)
    key = jax.random.fold_in(key, 11)
    least_tokens = max(MB_TOK - MB_TOK // 4, 1)
    tokens = jax.random.randint(key, (SECTIONS, POOL, SLOTS), least_tokens, MB_TOK + 1).astype(jnp.int32)
    slot_index = jnp.arange(SLOTS, dtype=jnp.int32)
    tokens = jnp.where(slot_index[None, None, :] == 0, MB_TOK, tokens)
    return jnp.where(slot_index[None, None, :] < live_count[:, :, None], tokens, 0).astype(jnp.int32)


def draw_route_ahead(key, part):
    live_count, forward_perm, backward_perm, offset_peer = wiring(key)
    return jax.vmap(lambda table, places: table[places])(forward_perm, offset_peer).astype(jnp.int32)


def draw_route_back(key, part):
    live_count, forward_perm, backward_perm, offset_peer = wiring(key)
    return jax.vmap(lambda table, places: table[places])(backward_perm, offset_peer).astype(jnp.int32)


def steps_of(own_key, extent, pieces, low, top_value):
    factor_of, own = 1.0, jax.random.fold_in(own_key, 6)
    for axis_at, shards_of in pieces:
        steps = jnp.exp(jax.random.uniform(jax.random.fold_in(own, axis_at), (shards_of,), jnp.float32, low / len(pieces), top_value / len(pieces)))
        factor_of = factor_of * jnp.repeat(steps, extent[axis_at] // shards_of).reshape([-1 if axis == axis_at else 1 for axis in range(len(extent))])
    return factor_of


def gaussian(own_key, extent, scale, bound, cuts=(), held_as=jnp.bfloat16):
    array = scale * jax.random.normal(own_key, extent, jnp.float32)
    if cuts:
        array = array * steps_of(own_key, extent, cuts, -0.22, 0.18)
    return jnp.clip(array, -bound, bound).astype(held_as)


def setup_inputs(seed: int = 0) -> dict:
    key_of = jax.random.split(jax.random.key(seed), 9)
    return {
        "activations": gaussian(key_of[0], (SECTIONS, POOL, SLOTS, MB_TOK, D), 1.0, 6.0, ((0, 8), (1, 64))),
        "cotangents": gaussian(key_of[1], (SECTIONS, POOL, SLOTS, MB_TOK, D), 1.0, 6.0, ((0, 8), (1, 64))),
        "token_counts": draw_token_counts(jax.random.fold_in(key_of[8], 71), 0),
        "route_ahead": draw_route_ahead(jax.random.fold_in(key_of[8], 71), 0),
        "route_back": draw_route_back(jax.random.fold_in(key_of[8], 71), 0),
        "down_rows": gaussian(key_of[5], (SECTIONS, R, D), D ** -0.5, 0.078125, ((0, 8), (1, 64))),
        "up_rows": gaussian(key_of[6], (SECTIONS, R, D), R ** -0.5, 0.75, ((0, 8), (1, 64))),
        "norm_gain": jnp.clip(1.0 + 0.18 * jax.random.normal(key_of[7], (SECTIONS, D), jnp.float32), 0.099609375, 1.8984375).astype(jnp.bfloat16),
    }


epsilon = 1e-05

def adapter_pass(section_in, grad_in, sizes, down_full, up_full, gain_row):
    slot_count, depth, width = section_in.shape
    row_ids = jnp.arange(depth, dtype=jnp.int32)
    keep_rows = (row_ids[None, :] < sizes[:, None]).reshape(slot_count * depth, 1)
    wide_in = section_in.reshape(slot_count * depth, width).astype(jnp.float32)
    gain_wide = gain_row.astype(jnp.float32)
    inv_rms = lax.rsqrt(lax.optimization_barrier(jnp.mean(wide_in * wide_in, axis=1, keepdims=True)) + epsilon)
    normed = (wide_in * inv_rms * gain_wide).astype(jnp.bfloat16)
    preact = lax.dot_general(normed, down_full, (((1,), (1,)), ((), ())), preferred_element_type=jnp.float32)
    gates = jax.nn.sigmoid(preact)
    hidden = (preact * gates).astype(jnp.bfloat16)
    branch = jnp.dot(hidden, up_full, preferred_element_type=jnp.float32)
    outward = jnp.where(keep_rows, wide_in + branch, 0.0).astype(jnp.bfloat16)
    grad_out = jnp.where(keep_rows, grad_in.reshape(slot_count * depth, width), jnp.zeros((), grad_in.dtype))
    grad_up = lax.dot_general(hidden, grad_out, (((0,), (0,)), ((), ())), preferred_element_type=jnp.float32)
    back_sum = lax.dot_general(grad_out, up_full, (((1,), (1,)), ((), ())), preferred_element_type=jnp.float32)
    slope_term = (back_sum * gates * (1.0 + preact * (1.0 - gates))).astype(jnp.bfloat16)
    grad_down = lax.dot_general(slope_term, normed, (((0,), (0,)), ((), ())), preferred_element_type=jnp.float32)
    through = jnp.dot(slope_term, down_full, preferred_element_type=jnp.float32) * gain_wide
    centred = lax.optimization_barrier(jnp.mean(through * wide_in, axis=1, keepdims=True))
    inward = (grad_out.astype(jnp.float32) + inv_rms * (through - wide_in * inv_rms * inv_rms * centred)).astype(jnp.bfloat16)
    return (outward.reshape(section_in.shape), inward.reshape(section_in.shape), grad_down, grad_up)

def pick_rows(values, sizes, targets, receiver):
    live_slots = (sizes > 0) & (targets == receiver)
    slot_ids = jnp.arange(sizes.shape[1], dtype=jnp.int32)
    out_ids = jnp.arange(CAP, dtype=jnp.int32)
    sender_ids = jnp.arange(sizes.shape[0], dtype=jnp.int32)
    which_slot = lax.optimization_barrier(jnp.sum(live_slots.astype(jnp.int32) * slot_ids[None, :], axis=1)).astype(jnp.int32)
    arrived = lax.optimization_barrier(jnp.sum(live_slots.astype(jnp.int32), axis=1)).astype(jnp.int32)
    chosen = values[sender_ids, which_slot]
    position = (jnp.cumsum(arrived) - 1).astype(jnp.int32)
    matched = (position[None, :] == out_ids[:, None]) & (arrived[None, :] > 0)
    source = lax.optimization_barrier(jnp.sum(matched.astype(jnp.int32) * sender_ids[None, :], axis=1)).astype(jnp.int32)
    valid_slot = jnp.any(matched, axis=1)
    return jnp.where(valid_slot[:, None, None], chosen[source], jnp.zeros((), values.dtype))

def reference(activations, cotangents, token_counts, route_ahead, route_back, down_rows, up_rows, norm_gain):

    def per_section(section_items):
        section_in, grad_in, sizes, ahead_to, back_to, down_full, up_full, gain_row = section_items
        outward, inward, grad_down, grad_up = jax.vmap(adapter_pass, in_axes=(0, 0, 0, None, None, None))(section_in, grad_in, sizes, down_full, up_full, gain_row)
        receivers = jnp.arange(section_in.shape[0], dtype=jnp.int32)
        forward_in = lax.map(lambda receiver: pick_rows(outward, sizes, ahead_to, receiver), receivers)
        behind = lax.map(lambda receiver: pick_rows(inward, sizes, back_to, receiver), receivers)
        return (forward_in, behind, lax.optimization_barrier(jnp.sum(grad_down, axis=0)), lax.optimization_barrier(jnp.sum(grad_up, axis=0)))
    forward_in, behind, grad_down, grad_up = lax.map(per_section, (activations, cotangents, token_counts, route_ahead, route_back, down_rows, up_rows, norm_gain))
    empty_section = jnp.zeros_like(forward_in[:1])
    arrived_ahead = jnp.concatenate([empty_section, forward_in[:-1]], axis=0)
    arrived_back = jnp.concatenate([behind[1:], empty_section], axis=0)
    return (arrived_ahead, arrived_back, grad_down, grad_up)
```

```python
import functools

import jax
import jax.numpy as jnp
from jax import lax
from jax.experimental import pallas as pl
from jax.experimental.pallas import tpu as pltpu
from jax.sharding import PartitionSpec as P

SLOTS = 12
TOK = 8
ROWS = SLOTS * TOK
N = 4
D = 5120
R = 64
NC = 5
CW = D // NC
LANE = 640
epsilon = 1e-05
MIB = 1 << 20


class Place:
    def __init__(self):
        section = lax.axis_index("section")
        pool = lax.axis_index("pool")
        self.section, self.pool = section, pool
        self.block, self.core = section // 2, section % 2
        self.x, self.y, self.z = pool // 16, (pool // 4) % 4, pool % 4

    def in_block(self, dx=0, dy=0, dz=0):
        x, y, z = (self.x + dx) % N, (self.y + dy) % N, (self.z + dz) % N
        return {"section": self.section, "pool": x * 16 + y * 4 + z}

    def sibling(self):
        return {"section": self.section + 1 - 2 * self.core, "pool": self.pool}

    def along_z(self, step):
        far = (self.block * N + self.z + step + 4 * N) % (4 * N)
        return {"section": (far // N) * 2 + self.core, "pool": self.pool - self.z + far % N}


def greet(peers):
    barrier = pltpu.get_barrier_semaphore()
    for peer in peers:
        pl.semaphore_signal(barrier, inc=1, device_id=peer, device_id_type=pl.DeviceIdType.MESH)
    pl.semaphore_wait(barrier, len(peers))


def remote(src, dst, send, recv, peer):
    return pltpu.make_async_remote_copy(
        src_ref=src, dst_ref=dst, send_sem=send, recv_sem=recv, device_id=peer, device_id_type=pl.DeviceIdType.MESH
    )


def gather_kernel(own_ref, table_ref, full_ref, tables_ref, local_sems, send_sems, recv_sems):
    me = Place()
    p, x, y, z = me.pool, me.x, me.y, me.z
    greet(
        [me.in_block(dz=1), me.in_block(dz=2), me.in_block(dz=3)]
        + [me.in_block(dy=1), me.in_block(dy=3), me.in_block(dx=1), me.in_block(dx=3)]
    )
    arrays = ((own_ref, full_ref), (table_ref, tables_ref))
    started = []

    def send(a, n, ref, start, count, peer):
        view = ref.at[pl.ds(start, count)]
        copy = remote(view, view, send_sems.at[a, n], recv_sems.at[a, n], peer)
        copy.start()
        started.append(copy)

    def arrive(a, n, ref, start, count, peer):
        view = ref.at[pl.ds(start, count)]
        remote(view, view, send_sems.at[a, n], recv_sems.at[a, n], peer).wait_recv()

    for a, (own, full) in enumerate(arrays):
        for d in (1, 2, 3):
            peer = me.in_block(dz=d)
            copy = remote(own, full.at[p], send_sems.at[a, d], recv_sems.at[a, d], peer)
            copy.start()
            started.append(copy)
        local = pltpu.make_async_copy(own, full.at[p], local_sems.at[a])
        local.start()
        local.wait()
    for a, (own, full) in enumerate(arrays):
        for d in (1, 2, 3):
            arrive(a, d, full, p - z + (z - d + N) % N, 1, me.in_block(dz=d))
    for first, count, coord, up, down in (
        (4, 4, y, me.in_block(dy=1), me.in_block(dy=3)),
        (8, 16, x, me.in_block(dx=1), me.in_block(dx=3)),
    ):
        base = (p // (count * N)) * (count * N)
        here = base + coord * count
        below = base + ((coord + 3) % N) * count
        above = base + ((coord + 1) % N) * count
        across = base + ((coord + 2) % N) * count
        half = count // 2
        for a, (_, full) in enumerate(arrays):
            send(a, first, full, here, count, up)
            send(a, first + 1, full, here, count, down)
        for a, (_, full) in enumerate(arrays):
            arrive(a, first, full, below, count, down)
            send(a, first + 2, full, below, half, up)
            arrive(a, first + 1, full, above, count, up)
            send(a, first + 3, full, above + half, half, down)
        for a, (_, full) in enumerate(arrays):
            arrive(a, first + 2, full, across, half, down)
            arrive(a, first + 3, full, across + half, half, up)
    for copy in started:
        copy.wait_send()


def gather(own, table):
    return pl.pallas_call(
        gather_kernel,
        out_shape=(
            jax.ShapeDtypeStruct((R, 16, LANE), jnp.bfloat16),
            jax.ShapeDtypeStruct((R, 8, 128), jnp.int32),
        ),
        in_specs=[pl.BlockSpec(memory_space=pltpu.VMEM)] * 2,
        out_specs=(pl.BlockSpec(memory_space=pltpu.VMEM),) * 2,
        scratch_shapes=[
            pltpu.SemaphoreType.DMA((2,)),
            pltpu.SemaphoreType.DMA((2, 12)),
            pltpu.SemaphoreType.DMA((2, 12)),
        ],
        compiler_params=pltpu.CompilerParams(
            collective_id=0, has_side_effects=True, vmem_limit_bytes=16 * MIB
        ),
        name="gather",
    )(own, table)


def adapter_kernel(x_ref, g_ref, keep_ref, down_ref, up_ref, gain_ref, routed_ref, gd_ref, gu_ref, normed, through):
    keep = keep_ref[...] > 0.0
    square = jnp.zeros((ROWS, 1), jnp.float32)
    for f in range(NC):
        wide = x_ref[:, f * CW : (f + 1) * CW].astype(jnp.float32)
        square += jnp.sum(wide * wide, axis=1, keepdims=True)
    inv_rms = lax.rsqrt(square * (1.0 / D) + epsilon)
    across = (((1,), (1,)), ((), ()))
    preact = jnp.zeros((ROWS, R), jnp.float32)
    back = jnp.zeros((ROWS, R), jnp.float32)
    for f in range(NC):
        cols = slice(f * CW, (f + 1) * CW)
        wide = x_ref[:, cols].astype(jnp.float32)
        part = (wide * inv_rms * gain_ref[:, cols].astype(jnp.float32)).astype(jnp.bfloat16)
        normed[:, cols] = part
        preact += lax.dot_general(part, down_ref[:, cols], across, preferred_element_type=jnp.float32)
        grad = jnp.where(keep, g_ref[:, cols].astype(jnp.float32), 0.0).astype(jnp.bfloat16)
        back += lax.dot_general(grad, up_ref[:, cols], across, preferred_element_type=jnp.float32)
    gates = jax.nn.sigmoid(preact)
    hidden_wide = (preact * gates).astype(jnp.bfloat16).astype(jnp.float32)
    slope_wide = (back * gates * (1.0 + preact * (1.0 - gates))).astype(jnp.bfloat16).astype(jnp.float32)
    hidden, slope = hidden_wide.astype(jnp.bfloat16), slope_wide.astype(jnp.bfloat16)
    hidden_t, slope_t = hidden_wide.T.astype(jnp.bfloat16), slope_wide.T.astype(jnp.bfloat16)
    centred = jnp.zeros((ROWS, 1), jnp.float32)
    for f in range(NC):
        cols = slice(f * CW, (f + 1) * CW)
        wide = x_ref[:, cols].astype(jnp.float32)
        branch = jnp.dot(hidden, up_ref[:, cols], preferred_element_type=jnp.float32)
        routed_ref[0, f] = jnp.where(keep, wide + branch, 0.0).astype(jnp.bfloat16)
        grad = jnp.where(keep, g_ref[:, cols].astype(jnp.float32), 0.0).astype(jnp.bfloat16)
        gu_ref[:, cols] = jnp.dot(hidden_t, grad, preferred_element_type=jnp.float32).astype(jnp.bfloat16)
        gd_ref[:, cols] = jnp.dot(slope_t, normed[:, cols], preferred_element_type=jnp.float32).astype(jnp.bfloat16)
        part = jnp.dot(slope, down_ref[:, cols], preferred_element_type=jnp.float32)
        part = part * gain_ref[:, cols].astype(jnp.float32)
        through[:, cols] = part
        centred += jnp.sum(part * wide, axis=1, keepdims=True)
    centred = centred * (1.0 / D)
    for f in range(NC):
        cols = slice(f * CW, (f + 1) * CW)
        wide = x_ref[:, cols].astype(jnp.float32)
        grad = jnp.where(keep, g_ref[:, cols].astype(jnp.float32), 0.0)
        inward = grad + inv_rms * (through[:, cols] - wide * inv_rms * inv_rms * centred)
        routed_ref[1, f] = inward.astype(jnp.bfloat16)


def adapter(rows, grads, keep, down_full, up_full, gain_row):
    whole = lambda shape: pl.BlockSpec(shape, lambda i: (0,) * len(shape))
    return pl.pallas_call(
        adapter_kernel,
        grid=(1,),
        out_shape=(
            jax.ShapeDtypeStruct((2, NC, ROWS, CW), jnp.bfloat16),
            jax.ShapeDtypeStruct((R, D), jnp.bfloat16),
            jax.ShapeDtypeStruct((R, D), jnp.bfloat16),
        ),
        in_specs=[
            whole((ROWS, D)),
            whole((ROWS, D)),
            whole((ROWS, 1)),
            whole((R, D)),
            whole((R, D)),
            whole((1, D)),
        ],
        out_specs=(whole((2, NC, ROWS, CW)), whole((R, D)), whole((R, D))),
        scratch_shapes=[pltpu.VMEM((ROWS, D), jnp.bfloat16), pltpu.VMEM((ROWS, D), jnp.float32)],
        compiler_params=pltpu.CompilerParams(vmem_limit_bytes=40 * MIB),
        cost_estimate=pl.CostEstimate(flops=6 * 2 * ROWS * R * D, bytes_accessed=10 * MIB, transcendentals=ROWS * R),
        name="adapter",
    )(rows, grads, keep, down_full, up_full, gain_row)


def repeat_matrix(rows, cols, times, along):
    r = lax.broadcasted_iota(jnp.int32, (rows, cols), 0)
    c = lax.broadcasted_iota(jnp.int32, (rows, cols), 1)
    return ((r // times == c) if along == 0 else (c // times == r)).astype(jnp.bfloat16)


def spread_tokens(small):
    a, b = small.shape
    tall = jnp.dot(repeat_matrix(TOK * a, a, TOK, 0), small, preferred_element_type=jnp.float32).astype(jnp.bfloat16)
    wide = jnp.dot(tall, repeat_matrix(b, TOK * b, TOK, 1), preferred_element_type=jnp.float32)
    r = lax.broadcasted_iota(jnp.int32, (TOK * a, TOK * b), 0) % TOK
    c = lax.broadcasted_iota(jnp.int32, (TOK * a, TOK * b), 1) % TOK
    return jnp.where(r == c, wide, 0.0).astype(jnp.bfloat16)


PAIR = N * N * TOK


def route_kernel(
    src, pick1, pick2, grads,
    ahead_out, behind_out, sums_out,
    lbuf, sbuf, dbuf, h1s, h1r, relay, h2s, mid, last, result, m1, m2,
    rs_mid, rs_send, rs_last, ry_src, ry_mid, ry_last, rz_src, rz_recv, total,
    lrecv, srecv, drecv, lup, ldn, ssend, dsend, swap_send,
    h1send, relay_in, relay_out, h1recv, far_send, mid_recv, near_send, last_recv, out_sem,
    rs_sems, rs_rsems, rz_sems, rz_rsems,
):
    me = Place()
    x, y, z, core = me.x, me.y, me.z, me.core
    o = jnp.where(core == 0, z, 3 - z)
    sibling = me.sibling()
    zup, zdown = me.in_block(dz=1), me.in_block(dz=3)
    znext = me.along_z(1 - 2 * core)
    zprev = me.along_z(2 * core - 1)
    xup, xdown, yup, ydown = me.in_block(dx=1), me.in_block(dx=3), me.in_block(dy=1), me.in_block(dy=3)
    greet([sibling, zup, me.in_block(dz=2), zdown, znext, zprev, xup, xdown, yup, ydown])

    def swap_local(f):
        return remote(src.at[core, f], lbuf.at[f, z], swap_send.at[0, f], lrecv.at[f, z], sibling)

    def swap_cross(f):
        so = 3 - o
        return remote(src.at[1 - core, f], sbuf.at[f, so], swap_send.at[1, f], srecv.at[f, so], sibling)

    def l_up(f, k):
        return remote(lbuf.at[f, k], lbuf.at[f, k], lup.at[f, k], lrecv.at[f, k], zup)

    def l_down(f, k):
        return remote(lbuf.at[f, k], lbuf.at[f, k], ldn.at[f, k], lrecv.at[f, k], zdown)

    def s_next(f, k):
        return remote(sbuf.at[f, k], sbuf.at[f, k], ssend.at[f, k], srecv.at[f, k], znext)

    def s_over(f, k):
        return remote(sbuf.at[f, k], dbuf.at[f, k], ssend.at[f, k], drecv.at[f, k], znext)

    def d_next(f, k):
        return remote(dbuf.at[f, k], dbuf.at[f, k], dsend.at[f, k], drecv.at[f, k], znext)

    half1, half2 = PAIR // 2, ROWS // 2

    def h1_near(r, f, d):
        n = 0 if d == 1 else 1
        return remote(
            h1s.at[r, f, d - 1], h1r.at[r, f, x], h1send.at[r, f, d - 1], h1recv.at[r, f, n], xup if d == 1 else xdown
        )

    def h1_far(r, f, way):
        part = pl.ds(way * half1, half1)
        return remote(
            h1s.at[r, f, 1, part], relay.at[way, r, f], h1send.at[r, f, 3 * way + 1], relay_in.at[way, r, f],
            xdown if way else xup,
        )

    def h1_relay(r, f, way):
        part = pl.ds(way * half1, half1)
        origin = (x + (1 if way else 3)) % N
        return remote(
            relay.at[way, r, f], h1r.at[r, f, origin, part], relay_out.at[way, r, f], h1recv.at[r, f, 2 + way],
            xdown if way else xup,
        )

    def h2_far(r, f, way):
        part = pl.ds(way * half2, half2)
        return remote(
            h2s.at[r, f, 2, part], mid.at[way, r, f], far_send.at[way, r, f], mid_recv.at[way, r, f],
            ydown if way else yup,
        )

    def h2_near(r, f, way):
        return remote(
            h2s.at[r, f, 3 if way else 1], last.at[way, r, f], near_send.at[way, r, f], last_recv.at[way, r, f],
            ydown if way else yup,
        )

    def emit(r, f, out):
        cols = pl.ds(pl.multiple_of(f * CW, 128), CW)
        return pltpu.make_async_copy(result.at[r, f], out.at[:, cols], out_sem.at[r, f])

    def z_begin(f):
        l_up(f, z).wait_recv()

        @pl.when(z < 3)
        def _():
            l_up(f, z).start()

        @pl.when(z > 0)
        def _():
            l_down(f, z).start()

        s_next(f, o).wait_recv()

        @pl.when(o < 3)
        def _():
            s_next(f, o).start()

        @pl.when(o == 3)
        def _():
            s_over(f, o).start()

    def z_rest(f):
        for t in range(1, 8):
            if t <= 3:

                @pl.when(z >= t)
                def _():
                    l_up(f, z - t).wait_recv()

                    @pl.when(z < 3)
                    def _():
                        l_up(f, z - t).start()

                @pl.when(z + t <= 3)
                def _():
                    l_down(f, z + t).wait_recv()

                    @pl.when(z > 0)
                    def _():
                        l_down(f, z + t).start()

                @pl.when(o >= t)
                def _():
                    s_next(f, o - t).wait_recv()

                    @pl.when(o < 3)
                    def _():
                        s_next(f, o - t).start()

                    @pl.when(o == 3)
                    def _():
                        s_over(f, o - t).start()

            @pl.when((o < t) & (t <= o + 4))
            def _():
                k = o + 4 - t
                d_next(f, k).wait_recv()

                @pl.when(o < 3)
                def _():
                    d_next(f, k).start()

    def h1_begin(f):
        for r, buf in ((0, lbuf), (1, dbuf)):
            block = buf[f].reshape(N * ROWS, CW)
            for d in (2, 1, 3, 0):
                to = (x + d) % N
                pick = m1[r, pl.ds(pl.multiple_of(to * PAIR, PAIR), PAIR), :]
                rows = jnp.dot(pick, block, preferred_element_type=jnp.float32).astype(jnp.bfloat16)
                if d == 0:
                    h1r[r, f, x] = rows
                else:
                    h1s[r, f, d - 1] = rows
                if d == 2:
                    h1_far(r, f, 0).start()
                    h1_far(r, f, 1).start()
                elif d:
                    h1_near(r, f, d).start()

    def h1_pass(f):
        for r in (0, 1):
            for way in (0, 1):
                h1_far(r, f, way).wait_recv()
                h1_relay(r, f, way).start()

    def h2_begin(f):
        for r in (0, 1):
            h1_near(r, f, 1).wait_recv()
            h1_near(r, f, 3).wait_recv()
            h1_relay(r, f, 0).wait_recv()
            h1_relay(r, f, 1).wait_recv()
            block = h1r[r, f].reshape(N * PAIR, CW)
            for e in (2, 1, 3, 0):
                to = (y + e) % N
                pick = m2[r, pl.ds(pl.multiple_of(to * ROWS, ROWS), ROWS), :]
                rows = jnp.dot(pick, block, preferred_element_type=jnp.float32).astype(jnp.bfloat16)
                h2s[r, f, e] = rows
                if e == 2:
                    h2_far(r, f, 0).start()
                    h2_far(r, f, 1).start()

    def h2_pass(f):
        for r in (0, 1):
            h2_far(r, f, 0).wait_recv()
            h2s[r, f, 1, :half2] = h2s[r, f, 1, :half2] + mid[0, r, f]
            h2_near(r, f, 0).start()
            h2_far(r, f, 1).wait_recv()
            h2s[r, f, 3, half2:] = h2s[r, f, 3, half2:] + mid[1, r, f]
            h2_near(r, f, 1).start()

    def finish(f):
        for r in (0, 1):
            h2_near(r, f, 0).wait_recv()
            h2_near(r, f, 1).wait_recv()
            result[r, f] = h2s[r, f, 0] + last[0, r, f] + last[1, r, f]

            @pl.when(core == 1 - r)
            def _():
                emit(r, f, ahead_out).start()

            @pl.when(core == r)
            def _():
                emit(r, f, behind_out).start()

    XR, YR = 16 * 16, 4 * 16

    def gsum_far(stage, buf, rows, across, coord, way):
        to = (coord + 2) % N
        dst = (rs_mid, ry_mid)[stage]
        return remote(
            buf.at[pl.ds(to * rows + way * (rows // 2), rows // 2)], dst.at[way],
            rs_sems.at[stage, way], rs_rsems.at[stage, way], across[way],
        )

    def gsum_near(stage, rows, across, way):
        dst = (rs_last, ry_last)[stage]
        return remote(
            rs_send.at[way, pl.ds(0, rows)], dst.at[way],
            rs_sems.at[stage, 2 + way], rs_rsems.at[stage, 2 + way], across[way],
        )

    xs, ys = (xup, xdown), (yup, ydown)

    def gsum_pass(stage, buf, rows, across, coord):
        dst = (rs_mid, ry_mid)[stage]
        h = rows // 2
        for way in (0, 1):
            if stage == 1:
                gsum_near(0, XR, xs, way).wait_send()
            gsum_far(stage, buf, rows, across, coord, way).wait_recv()
            to = (coord + (3 if way else 1)) % N
            base = pl.multiple_of(to * rows, 32)
            first = buf[pl.ds(base, h), :]
            second = buf[pl.ds(pl.multiple_of(base + h, 32), h), :]
            far = dst[way].astype(jnp.float32)
            if way == 0:
                first = (first.astype(jnp.float32) + far).astype(jnp.bfloat16)
            else:
                second = (second.astype(jnp.float32) + far).astype(jnp.bfloat16)
            rs_send[way, pl.ds(0, h), :] = first
            rs_send[way, pl.ds(h, h), :] = second
            gsum_near(stage, rows, across, way).start()

    def gsum_total(stage, buf, rows, across, coord):
        dst = (rs_last, ry_last)[stage]
        for way in (0, 1):
            gsum_near(stage, rows, across, way).wait_recv()
        own = buf[pl.ds(pl.multiple_of(coord * rows, 32), rows), :].astype(jnp.float32)
        return own + dst[0].astype(jnp.float32) + dst[1].astype(jnp.float32)

    def gsum_z(d):
        to = (z + d) % N
        return remote(
            rz_src.at[pl.ds(to * 16, 16)], rz_recv.at[z], rz_sems.at[d], rz_rsems.at[z], me.in_block(dz=d)
        )

    def gsum_z_arrival(d):
        origin = (z + d) % N
        return remote(
            rz_src.at[pl.ds(0, 16)], rz_recv.at[origin], rz_sems.at[d], rz_rsems.at[origin], me.in_block(dz=d)
        )

    def swap(f, _):
        swap_local(f).start()
        swap_cross(f).start()
        return 0

    lax.fori_loop(0, NC, swap, 0)
    gsum_far(0, grads, XR, xs, x, 0).start()
    gsum_far(0, grads, XR, xs, x, 1).start()
    for r in (0, 1):
        m1[r] = spread_tokens(pick1[r])
        m2[r] = spread_tokens(pick2[r])
    z_begin(0)

    def step(n, _):
        @pl.when(n + 1 < NC)
        def _():
            z_begin(n + 1)

        @pl.when(n < NC)
        def _():
            z_rest(n)
            h1_begin(n)

        @pl.when((n >= 1) & (n < NC + 1))
        def _():
            h1_pass(n - 1)

        @pl.when(n == 0)
        def _():
            gsum_pass(0, grads, XR, xs, x)

        @pl.when(n == 1)
        def _():
            ry_src[...] = gsum_total(0, grads, XR, xs, x).astype(jnp.bfloat16)
            gsum_far(1, ry_src, YR, ys, y, 0).start()
            gsum_far(1, ry_src, YR, ys, y, 1).start()

        @pl.when(n == 2)
        def _():
            gsum_pass(1, ry_src, YR, ys, y)

        @pl.when(n == 3)
        def _():
            both = gsum_total(1, ry_src, YR, ys, y)
            rz_src[...] = both.astype(jnp.bfloat16)
            total[...] = both
            for d in (1, 2, 3):
                gsum_z(d).start()

        @pl.when((n >= 2) & (n < NC + 2))
        def _():
            h2_pass(n - 2)

        @pl.when((n >= 1) & (n < NC + 1))
        def _():
            h2_begin(n - 1)

        @pl.when(n >= 3)
        def _():
            finish(n - 3)

        return 0

    lax.fori_loop(0, NC + 3, step, 0)

    acc = total[pl.ds(pl.multiple_of(z * 16, 16), 16), :]
    for d in (1, 2, 3):
        gsum_z_arrival(d).wait_recv()
        acc = acc + rz_recv[(z + d) % N].astype(jnp.float32)
    sums_out[...] = acc

    for way in (0, 1):
        gsum_far(0, grads, XR, xs, x, way).wait_send()
        gsum_far(1, ry_src, YR, ys, y, way).wait_send()
        gsum_near(1, YR, ys, way).wait_send()
    for d in (1, 2, 3):
        gsum_z(d).wait_send()

    def drain(f, _):
        swap_local(f).wait_send()
        swap_cross(f).wait_send()
        for k in range(N):

            @pl.when((z < 3) & (k <= z))
            def _():
                l_up(f, k).wait_send()

            @pl.when((z > 0) & (k >= z))
            def _():
                l_down(f, k).wait_send()

            @pl.when(k <= o)
            def _():
                s_next(f, k).wait_send()

            @pl.when(o < 3)
            def _():
                d_next(f, k).wait_send()

        for r in (0, 1):
            h1_near(r, f, 1).wait_send()
            h1_near(r, f, 3).wait_send()
            for way in (0, 1):
                h1_far(r, f, way).wait_send()
                h1_relay(r, f, way).wait_send()
                h2_far(r, f, way).wait_send()
                h2_near(r, f, way).wait_send()
            emit(r, f, ahead_out).wait()
        return 0

    lax.fori_loop(0, NC, drain, 0)


def route(routed, pick1, pick2, grads):
    bf16, f32 = jnp.bfloat16, jnp.float32
    vmem, dma = pltpu.VMEM, pltpu.SemaphoreType.DMA
    scratch = [
        vmem((NC, N, ROWS, CW), bf16),
        vmem((NC, N, ROWS, CW), bf16),
        vmem((NC, N, ROWS, CW), bf16),
        vmem((2, NC, 3, PAIR, CW), bf16),
        vmem((2, NC, N, PAIR, CW), bf16),
        vmem((2, 2, NC, PAIR // 2, CW), bf16),
        vmem((2, NC, N, ROWS, CW), bf16),
        vmem((2, 2, NC, ROWS // 2, CW), bf16),
        vmem((2, 2, NC, ROWS, CW), bf16),
        vmem((2, NC, ROWS, CW), bf16),
        vmem((2, N * PAIR, N * ROWS), bf16),
        vmem((2, N * ROWS, N * PAIR), bf16),
        vmem((2, 128, LANE), bf16),
        vmem((2, 256, LANE), bf16),
        vmem((2, 256, LANE), bf16),
        vmem((256, LANE), bf16),
        vmem((2, 32, LANE), bf16),
        vmem((2, 64, LANE), bf16),
        vmem((64, LANE), bf16),
        vmem((N, 16, LANE), bf16),
        vmem((64, LANE), f32),
        dma((NC, N)), dma((NC, N)), dma((NC, N)),
        dma((NC, N)), dma((NC, N)), dma((NC, N)), dma((NC, N)),
        dma((2, NC)),
        dma((2, NC, 5)),
        dma((2, 2, NC)), dma((2, 2, NC)),
        dma((2, NC, 4)),
        dma((2, 2, NC)), dma((2, 2, NC)),
        dma((2, 2, NC)), dma((2, 2, NC)),
        dma((2, NC)),
        dma((2, 4)), dma((2, 4)), dma((N,)), dma((N,)),
    ]
    return pl.pallas_call(
        route_kernel,
        out_shape=(
            jax.ShapeDtypeStruct((ROWS, D), bf16),
            jax.ShapeDtypeStruct((ROWS, D), bf16),
            jax.ShapeDtypeStruct((16, LANE), f32),
        ),
        in_specs=[pl.BlockSpec(memory_space=pltpu.VMEM)] * 4,
        out_specs=(
            pl.BlockSpec(memory_space=pl.ANY),
            pl.BlockSpec(memory_space=pl.ANY),
            pl.BlockSpec(memory_space=pltpu.VMEM),
        ),
        scratch_shapes=scratch,
        compiler_params=pltpu.CompilerParams(
            collective_id=1, has_side_effects=True, vmem_limit_bytes=62 * MIB
        ),
        name="route",
    )(routed, pick1, pick2, grads)


def picks(tables, flip):
    me = Place()
    column = lax.dynamic_slice(tables, (me.x * 16 + me.y * 4, 0), (N, SLOTS))
    to = jnp.arange(N * N, dtype=jnp.int32) * 4 + me.z + 1
    source = jnp.arange(N, dtype=jnp.int32)
    place = jnp.where(flip, 3 - source, source)
    hit = column[None, :, None, :] == to[:, None, None, None]
    first = hit & (place[:, None] == source[None, :])[None, :, :, None]
    mine = me.x * 16 + jnp.arange(N, dtype=jnp.int32) * 4 + me.z + 1
    sent = jnp.any(tables[None] == mine[:, None, None], axis=2)
    spot = jnp.cumsum(sent.astype(jnp.int32), axis=1) - 1
    spot = jnp.where(sent, spot, -1).reshape(N, N, N, N)
    spot = lax.dynamic_index_in_dim(spot, me.y, 2, keepdims=False)
    slot = jnp.arange(SLOTS, dtype=jnp.int32)
    second = spot[:, None, :, None, :] == slot[None, :, None, None, None]
    second = second & (source[:, None] == source[None, :])[:, None, None, :, None]
    return (
        first.reshape(N * N * N, N * SLOTS).astype(jnp.bfloat16),
        second.reshape(N * SLOTS, N * N * N).astype(jnp.bfloat16),
    )


def shards(
    activations, cotangents, token_counts, route_ahead, route_back, down_rows, up_rows, norm_gain
):
    sizes = token_counts[0, 0, :SLOTS]
    live = sizes > 0
    entry = jnp.stack(
        [jnp.where(live, route_ahead[0, 0, :SLOTS] + 1, 0), jnp.where(live, route_back[0, 0, :SLOTS] + 1, 0)]
    )
    table = jnp.zeros((8, 128), jnp.int32).at[:2, :SLOTS].set(entry)
    own = jnp.concatenate([down_rows[0, 0].reshape(8, LANE), up_rows[0, 0].reshape(8, LANE)], axis=0)
    full, tables = gather(own, table)
    down_full, up_full = full[:, :8].reshape(R, D), full[:, 8:].reshape(R, D)
    count = lax.axis_size("section")
    from_prev = lax.ppermute(tables[:, 0, :SLOTS], "section", [(s, s + 1) for s in range(count - 1)])
    from_next = lax.ppermute(tables[:, 1, :SLOTS], "section", [(s + 1, s) for s in range(count - 1)])

    rows = activations.reshape(-1, D)
    grads = cotangents.reshape(-1, D)
    keep = (jnp.arange(TOK, dtype=jnp.int32)[None, :] < sizes[:, None]).astype(jnp.float32).reshape(ROWS, 1)
    routed, grad_down, grad_up = adapter(rows, grads, keep, down_full, up_full, norm_gain)

    odd = lax.axis_index("section") % 2 == 1
    local, cross = jnp.where(odd, from_prev, from_next), jnp.where(odd, from_next, from_prev)
    local1, local2 = picks(local, False)
    cross1, cross2 = picks(cross, odd)
    share = jnp.concatenate([grad_down.reshape(R, 8, LANE), grad_up.reshape(R, 8, LANE)], axis=1)
    ahead, behind, sums = route(
        routed, jnp.stack([local1, cross1]), jnp.stack([local2, cross2]), share.reshape(R * 16, LANE)
    )
    shape = (1, 1, SLOTS, TOK, D)
    sums = sums.reshape(2, 1, 1, D)
    return (ahead.reshape(shape), behind.reshape(shape), sums[0], sums[1])


def solution(mesh):
    placed = (
        P("section", "pool", None, None, None),
        P("section", "pool", None, None, None),
        P("section", "pool", None),
        P("section", "pool", None),
        P("section", "pool", None),
        P("section", "pool", None),
        P("section", "pool", None),
        P("section", None),
    )
    return jax.shard_map(
        shards,
        mesh=mesh,
        in_specs=placed,
        out_specs=(
            P("section", "pool", None, None, None),
            P("section", "pool", None, None, None),
            P("section", "pool", None),
            P("section", "pool", None),
        ),
        check_vma=False,
    )
```

```python
import functools

import jax
import jax.numpy as jnp
from jax import lax
from jax.experimental import pallas as pl
from jax.experimental.pallas import tpu as pltpu
from jax.sharding import PartitionSpec as P

SLOTS = 12
TOK = 8
ROWS = SLOTS * TOK
N = 4
D = 5120
R = 64
NC = 5
CW = D // NC
LANE = 640
epsilon = 1e-05
MIB = 1 << 20


class Place:
    def __init__(self):
        section = lax.axis_index("section")
        pool = lax.axis_index("pool")
        self.section, self.pool = section, pool
        self.block, self.core = section // 2, section % 2
        self.x, self.y, self.z = pool // 16, (pool // 4) % 4, pool % 4

    def in_block(self, dx=0, dy=0, dz=0):
        x, y, z = (self.x + dx) % N, (self.y + dy) % N, (self.z + dz) % N
        return {"section": self.section, "pool": x * 16 + y * 4 + z}

    def along_z(self, step):
        far = (self.block * N + self.z + step + 4 * N) % (4 * N)
        return {"section": (far // N) * 2 + self.core, "pool": self.pool - self.z + far % N}


def greet(peers):
    barrier = pltpu.get_barrier_semaphore()
    for peer in peers:
        pl.semaphore_signal(barrier, inc=1, device_id=peer, device_id_type=pl.DeviceIdType.MESH)
    pl.semaphore_wait(barrier, len(peers))


def remote(src, dst, send, recv, peer):
    return pltpu.make_async_remote_copy(
        src_ref=src, dst_ref=dst, send_sem=send, recv_sem=recv, device_id=peer, device_id_type=pl.DeviceIdType.MESH
    )


def gather_kernel(own_ref, table_ref, full_ref, tables_ref, tin, local_sems, tin_send, tin_recv, send_sems, recv_sems):
    me = Place()
    x, y, z = me.x, me.y, me.z
    others = (1, 2, 3)
    to_next = {"section": (me.section + 1) % 8, "pool": me.pool}
    to_prev = {"section": (me.section + 7) % 8, "pool": me.pool}
    along = {
        "x": {d: me.in_block(dx=d) for d in others},
        "y": {d: me.in_block(dy=d) for d in others},
        "z": {d: me.in_block(dz=d) for d in others},
    }
    greet([to_next, to_prev] + [along[axis][d] for axis in "xyz" for d in others])

    crossing = [
        remote(table_ref.at[pl.ds(0, 16)], tin.at[pl.ds(0, 16)], tin_send.at[0], tin_recv.at[0], to_next),
        remote(table_ref.at[pl.ds(16, 16)], tin.at[pl.ds(16, 16)], tin_send.at[1], tin_recv.at[1], to_prev),
    ]
    for copy in crossing:
        copy.start()

    half, k = z // 2, z % 2
    place = jnp.where(half == 0, x * 8 + y * 2, y * 8 + x * 2)
    started = []

    def spread(a, own, full):
        for d in others:
            copy = remote(own, full.at[half, place + k], send_sems.at[a, d], recv_sems.at[a, z], along["z"][d])
            copy.start()
            started.append(copy)
        local = pltpu.make_async_copy(own, full.at[half, place + k], local_sems.at[a])
        local.start()
        local.wait()

    def collect(a, own, full):
        for d in others:
            origin = (z + d) % N
            h, kk = origin // 2, origin % 2
            here = jnp.where(h == 0, x * 8 + y * 2, y * 8 + x * 2) + kk
            remote(own, full.at[h, here], send_sems.at[a, d], recv_sems.at[a, origin], along["z"][d]).wait_recv()

    def stage(a, full, n, wait):
        for h in (0, 1):
            first, second = ((y, x), (x, y))[h]
            axis = ("yx", "xy")[h][n]
            for d in others:
                size = 2 if n == 0 else 8
                at = (second * 8 + first * 2) if n == 0 else second * 8
                sem = 4 + h * 6 + n * 3 + d - 1
                if wait:
                    at = (second * 8 + ((first - d + N) % N) * 2) if n == 0 else ((second - d + N) % N) * 8
                view = full.at[h, pl.ds(at, size)]
                copy = remote(view, view, send_sems.at[a, sem], recv_sems.at[a, sem], along[axis][d])
                if wait:
                    copy.wait_recv()
                else:
                    copy.start()
                    started.append(copy)

    weights = (0, own_ref, full_ref)
    marks = (1, tin, tables_ref)
    spread(*weights)
    for copy in crossing:
        copy.wait_recv()
    spread(*marks)
    collect(*weights)
    stage(0, full_ref, 0, False)
    collect(*marks)
    stage(1, tables_ref, 0, False)
    stage(0, full_ref, 0, True)
    stage(0, full_ref, 1, False)
    stage(1, tables_ref, 0, True)
    stage(1, tables_ref, 1, False)
    stage(0, full_ref, 1, True)
    stage(1, tables_ref, 1, True)
    for copy in crossing + started:
        copy.wait_send()


def gather(own, table):
    dma = pltpu.SemaphoreType.DMA
    return pl.pallas_call(
        gather_kernel,
        out_shape=(
            jax.ShapeDtypeStruct((2, R // 2, 16, LANE), jnp.bfloat16),
            jax.ShapeDtypeStruct((2, R // 2, 32, 128), jnp.bfloat16),
        ),
        in_specs=[pl.BlockSpec(memory_space=pltpu.VMEM)] * 2,
        out_specs=(pl.BlockSpec(memory_space=pltpu.VMEM),) * 2,
        scratch_shapes=[
            pltpu.VMEM((32, 128), jnp.bfloat16), dma((2,)), dma((2,)), dma((2,)), dma((2, 16)), dma((2, 16)),
        ],
        compiler_params=pltpu.CompilerParams(
            collective_id=0, has_side_effects=True, vmem_limit_bytes=16 * MIB
        ),
        name="gather",
    )(own, table)


def adapter_kernel(x_ref, g_ref, keep_ref, down_ref, up_ref, gain_ref, routed_ref, gd_ref, gu_ref, normed, through):
    keep = keep_ref[...] > 0.0
    square = jnp.zeros((ROWS, 1), jnp.float32)
    for f in range(NC):
        wide = x_ref[:, f * CW : (f + 1) * CW].astype(jnp.float32)
        square += jnp.sum(wide * wide, axis=1, keepdims=True)
    inv_rms = lax.rsqrt(square * (1.0 / D) + epsilon)
    across = (((1,), (1,)), ((), ()))
    preact = jnp.zeros((ROWS, R), jnp.float32)
    back = jnp.zeros((ROWS, R), jnp.float32)
    for f in range(NC):
        cols = slice(f * CW, (f + 1) * CW)
        wide = x_ref[:, cols].astype(jnp.float32)
        part = (wide * inv_rms * gain_ref[:, cols].astype(jnp.float32)).astype(jnp.bfloat16)
        normed[:, cols] = part
        preact += lax.dot_general(part, down_ref[:, cols], across, preferred_element_type=jnp.float32)
        grad = jnp.where(keep, g_ref[:, cols].astype(jnp.float32), 0.0).astype(jnp.bfloat16)
        back += lax.dot_general(grad, up_ref[:, cols], across, preferred_element_type=jnp.float32)
    gates = jax.nn.sigmoid(preact)
    hidden_wide = (preact * gates).astype(jnp.bfloat16).astype(jnp.float32)
    slope_wide = (back * gates * (1.0 + preact * (1.0 - gates))).astype(jnp.bfloat16).astype(jnp.float32)
    hidden, slope = hidden_wide.astype(jnp.bfloat16), slope_wide.astype(jnp.bfloat16)
    hidden_t, slope_t = hidden_wide.T.astype(jnp.bfloat16), slope_wide.T.astype(jnp.bfloat16)
    centred = jnp.zeros((ROWS, 1), jnp.float32)
    for f in range(NC):
        cols = slice(f * CW, (f + 1) * CW)
        wide = x_ref[:, cols].astype(jnp.float32)
        branch = jnp.dot(hidden, up_ref[:, cols], preferred_element_type=jnp.float32)
        routed_ref[0, f] = jnp.where(keep, wide + branch, 0.0).astype(jnp.bfloat16)
        grad = jnp.where(keep, g_ref[:, cols].astype(jnp.float32), 0.0).astype(jnp.bfloat16)
        gu_ref[:, cols] = jnp.dot(hidden_t, grad, preferred_element_type=jnp.float32).astype(jnp.bfloat16)
        gd_ref[:, cols] = jnp.dot(slope_t, normed[:, cols], preferred_element_type=jnp.float32).astype(jnp.bfloat16)
        part = jnp.dot(slope, down_ref[:, cols], preferred_element_type=jnp.float32)
        part = part * gain_ref[:, cols].astype(jnp.float32)
        through[:, cols] = part
        centred += jnp.sum(part * wide, axis=1, keepdims=True)
    centred = centred * (1.0 / D)
    for f in range(NC):
        cols = slice(f * CW, (f + 1) * CW)
        wide = x_ref[:, cols].astype(jnp.float32)
        grad = jnp.where(keep, g_ref[:, cols].astype(jnp.float32), 0.0)
        inward = grad + inv_rms * (through[:, cols] - wide * inv_rms * inv_rms * centred)
        routed_ref[1, f] = inward.astype(jnp.bfloat16)


def adapter(rows, grads, keep, down_full, up_full, gain_row):
    whole = lambda shape: pl.BlockSpec(shape, lambda i: (0,) * len(shape))
    return pl.pallas_call(
        adapter_kernel,
        grid=(1,),
        out_shape=(
            jax.ShapeDtypeStruct((2, NC, ROWS, CW), jnp.bfloat16),
            jax.ShapeDtypeStruct((R, D), jnp.bfloat16),
            jax.ShapeDtypeStruct((R, D), jnp.bfloat16),
        ),
        in_specs=[
            whole((ROWS, D)),
            whole((ROWS, D)),
            whole((ROWS, 1)),
            whole((R, D)),
            whole((R, D)),
            whole((1, D)),
        ],
        out_specs=(whole((2, NC, ROWS, CW)), whole((R, D)), whole((R, D))),
        scratch_shapes=[pltpu.VMEM((ROWS, D), jnp.bfloat16), pltpu.VMEM((ROWS, D), jnp.float32)],
        compiler_params=pltpu.CompilerParams(vmem_limit_bytes=40 * MIB),
        cost_estimate=pl.CostEstimate(flops=6 * 2 * ROWS * R * D, bytes_accessed=10 * MIB, transcendentals=ROWS * R),
        name="adapter",
    )(rows, grads, keep, down_full, up_full, gain_row)


def repeat_matrix(rows, cols, times, along):
    r = lax.broadcasted_iota(jnp.int32, (rows, cols), 0)
    c = lax.broadcasted_iota(jnp.int32, (rows, cols), 1)
    return ((r // times == c) if along == 0 else (c // times == r)).astype(jnp.bfloat16)


def spread_tokens(small):
    a, b = small.shape
    tall = jnp.dot(repeat_matrix(TOK * a, a, TOK, 0), small, preferred_element_type=jnp.float32).astype(jnp.bfloat16)
    wide = jnp.dot(tall, repeat_matrix(b, TOK * b, TOK, 1), preferred_element_type=jnp.float32)
    r = lax.broadcasted_iota(jnp.int32, (TOK * a, TOK * b), 0) % TOK
    c = lax.broadcasted_iota(jnp.int32, (TOK * a, TOK * b), 1) % TOK
    return jnp.where(r == c, wide, 0.0).astype(jnp.bfloat16)


PAIR = N * N * TOK
AHEAD = 2


def route_kernel(
    src, pick1, pick2, grads,
    ahead_out, behind_out, sums_out,
    lbuf, dbuf, h1s, h1r, h2s, last, zpart, result, m1, m2,
    g1, g1_sum, g2, g3, total,
    lsend, lrecv, xsend, drecv, dsend, h1send, h1recv, h2send, h2recv, zsend, zrecv, out_sem,
    gsend, grecv,
):
    me = Place()
    x, y, z, core = me.x, me.y, me.z, me.core
    o = jnp.where(core == 0, z, 3 - z)
    znext = me.along_z(1 - 2 * core)
    others = (1, 2, 3)
    along = {"x": {d: me.in_block(dx=d) for d in others}, "y": {d: me.in_block(dy=d) for d in others}}
    zup, zdown = me.in_block(dz=1), me.in_block(dz=3)
    other_core = me.section + 1 - 2 * core

    def facing(d):
        return {"section": other_core, "pool": ((x + d) % N) * 16 + y * 4 + z}

    entry = {
        "section": ((me.block + 2 * core - 1 + N) % N) * 2 + 1 - core,
        "pool": me.pool - z + 3 * (1 - core),
    }
    so = jnp.where(core == 1, z, 3 - z)

    barrier = pltpu.get_barrier_semaphore()

    def hello(peer):
        pl.semaphore_signal(barrier, inc=1, device_id=peer, device_id_type=pl.DeviceIdType.MESH)

    everyone = [me.in_block(dz=d) for d in others] + [along["x"][d] for d in others] + [along["y"][d] for d in others]
    everyone += [znext, me.along_z(2 * core - 1)]
    everyone += [facing(d) for d in range(N)]
    for way in (1, N - 1):
        for k in range(N):
            everyone.append({"section": ((me.block + way) % N) * 2 + 1 - core, "pool": me.pool - z + k})
    for peer in everyone:
        hello(peer)
    pl.semaphore_wait(barrier, len(everyone))

    def local_copy(f, d):
        return remote(src.at[core, f], lbuf.at[f, x], lsend.at[f, d], lrecv.at[f, d], facing(d))

    def cross_copy(f):
        return remote(src.at[1 - core, f], dbuf.at[f, so], xsend.at[f], drecv.at[f, so], entry)

    def cross_pass(f, k):
        return remote(dbuf.at[f, k], dbuf.at[f, k], dsend.at[f, k], drecv.at[f, k], znext)

    def h1_copy(r, f, d):
        return remote(
            h1s.at[r, f, d - 1], h1r.at[r, f, x if r else y], h1send.at[r, f, d - 1], h1recv.at[r, f, d - 1],
            along["x" if r else "y"][d],
        )

    def h2_copy(f, d):
        return remote(h2s.at[1, f, d], last.at[f, d - 1], h2send.at[f, d - 1], h2recv.at[f, d - 1], along["y"][d])

    def z_copy(f, to, way):
        slot = (z - to - 1) if way else (to - z - 1)
        return remote(
            h2s.at[0, f, to], zpart.at[f, way, slot], zsend.at[f, to], zrecv.at[f, way, slot], zdown if way else zup
        )

    def z_arrival(f, slot, way):
        return remote(
            h2s.at[0, f, 0], zpart.at[f, way, slot], zsend.at[f, 0], zrecv.at[f, way, slot], zdown if way else zup
        )

    def emit(r, f, out):
        cols = pl.ds(pl.multiple_of(f * CW, 128), CW)
        return pltpu.make_async_copy(result.at[r, f], out.at[:, cols], out_sem.at[r, f])

    def z_begin(f):
        cross_copy(f).start()
        for d in (2, 1, 3, 0):
            local_copy(f, d).start()

    def z_rest(f):
        for k in (3, 2, 1, 0):
            cross_pass(f, k).wait_recv()

            @pl.when(o < 3)
            def _():
                cross_pass(f, k).start()

    def h1_begin(r, f):
        if r == 0:
            for d in range(N):
                local_copy(f, d).wait_recv()
        here = x if r else y
        block = (dbuf if r else lbuf)[f].reshape(N * ROWS, CW)
        for d in (2, 1, 3, 0):
            to = (here + d) % N
            pick = m1[r, pl.ds(pl.multiple_of(to * PAIR, PAIR), PAIR), :]
            rows = jnp.dot(pick, block, preferred_element_type=jnp.float32).astype(jnp.bfloat16)
            if d == 0:
                h1r[r, f, here] = rows
            else:
                h1s[r, f, d - 1] = rows
                h1_copy(r, f, d).start()

    def h2_begin(r, f):
        for d in others:
            h1_copy(r, f, d).wait_recv()
        block = h1r[r, f].reshape(N * PAIR, CW)
        for d in (2, 1, 3, 0):
            to = (y + d) % N if r else d
            pick = m2[r, pl.ds(pl.multiple_of(to * ROWS, ROWS), ROWS), :]
            h2s[r, f, d] = jnp.dot(pick, block, preferred_element_type=jnp.float32).astype(jnp.bfloat16)
            if r and d:
                h2_copy(f, d).start()
        if r == 0:

            @pl.when(z == 0)
            def _():
                for to in (3, 2, 1):
                    z_copy(f, to, 0).start()

            @pl.when(z == 3)
            def _():
                for to in (0, 1, 2):
                    z_copy(f, to, 1).start()

    def add_on(f, to, way):
        slot = (z - to) if way else (to - z)
        z_arrival(f, slot, way).wait_recv()
        h2s[0, f, to] = h2s[0, f, to] + zpart[f, way, slot]
        z_copy(f, to, way).start()

    def merge_first(f):
        @pl.when(z == 1)
        def _():
            add_on(f, 3, 0)
            add_on(f, 2, 0)

        @pl.when(z == 2)
        def _():
            add_on(f, 0, 1)
            add_on(f, 1, 1)

    def merge_second(f):
        @pl.when(z == 2)
        def _():
            add_on(f, 3, 0)

        @pl.when(z == 1)
        def _():
            add_on(f, 0, 1)

    def hand_out(r, f):
        @pl.when(core == 1 - r)
        def _():
            emit(r, f, ahead_out).start()

        @pl.when(core == r)
        def _():
            emit(r, f, behind_out).start()

    def finish_local(f):
        result[0, f] = h2s[0, f, z]

        @pl.when(z > 0)
        def _():
            z_arrival(f, 0, 0).wait_recv()
            result[0, f] = result[0, f] + zpart[f, 0, 0]

        @pl.when(z < 3)
        def _():
            z_arrival(f, 0, 1).wait_recv()
            result[0, f] = result[0, f] + zpart[f, 1, 0]

        hand_out(0, f)

    def finish_cross(f):
        for d in others:
            h2_copy(f, d).wait_recv()
        result[1, f] = (h2s[1, f, 0] + last[f, 0]) + (last[f, 1] + last[f, 2])
        hand_out(1, f)

    G1, G2, G3 = 128, 32, 16

    def axis_of(n, h):
        return "xy"[(n + h) % 2]

    def at(axis):
        return x if axis == "x" else y

    def g1_copy(h, d):
        axis = axis_of(0, h)
        to = (at(axis) + d) % N
        return remote(
            grads.at[pl.ds(h * 512 + to * G1, G1)], g1.at[h, d - 1], gsend.at[0, h, d - 1], grecv.at[0, h, d - 1],
            along[axis][d],
        )

    def g2_copy(h, d):
        axis = axis_of(1, h)
        to = (at(axis) + d) % N
        return remote(
            g1_sum.at[h, pl.ds(to * G2, G2)], g2.at[h, d - 1], gsend.at[1, h, d - 1], grecv.at[1, h, d - 1],
            along[axis][d],
        )

    def g3_copy(d):
        to = (z + d) % N
        return remote(
            total.at[pl.ds(to * G3, G3)], g3.at[d - 1], gsend.at[2, 0, d - 1], grecv.at[2, 0, d - 1], me.in_block(dz=d)
        )

    def add_three(own, parts):
        return (own + parts[0].astype(jnp.float32)) + (parts[1].astype(jnp.float32) + parts[2].astype(jnp.float32))

    def grads_first():
        for h in (0, 1):
            for d in others:
                g1_copy(h, d).start()

    def grads_second():
        for h in (0, 1):
            for d in others:
                g1_copy(h, d).wait_recv()
            row = pl.multiple_of(h * 512 + at(axis_of(0, h)) * G1, G1)
            g1_sum[h] = add_three(grads[pl.ds(row, G1), :].astype(jnp.float32), g1[h])
            for d in others:
                g2_copy(h, d).start()

    def grads_third():
        for h in (0, 1):
            for d in others:
                g2_copy(h, d).wait_recv()
            row = pl.multiple_of(at(axis_of(1, h)) * G2, G2)
            total[pl.ds(h * G2, G2), :] = add_three(g1_sum[h, pl.ds(row, G2), :], g2[h])
        for d in others:
            g3_copy(d).start()

    def grads_last():
        for d in others:
            g3_copy(d).wait_recv()
        sums_out[...] = add_three(total[pl.ds(pl.multiple_of(z * G3, G3), G3), :], g3[...])

    for f in range(AHEAD):
        z_begin(f)
    grads_first()
    for r in (0, 1):
        m1[r] = spread_tokens(pick1[r])
        m2[r] = spread_tokens(pick2[r])

    def when_chunk(n, lag, run):
        pl.when((n >= lag) & (n < NC + lag))(lambda: run(n - lag))

    def step(n, _):
        when_chunk(n, -AHEAD, z_begin)
        when_chunk(n, 0, lambda f: h1_begin(0, f))
        when_chunk(n, 2, merge_first)
        when_chunk(n, 3, merge_second)
        when_chunk(n, 0, z_rest)
        when_chunk(n, 0, lambda f: h1_begin(1, f))
        when_chunk(n, 1, lambda f: h2_begin(0, f))
        pl.when(n == 1)(grads_second)
        pl.when(n == 2)(grads_third)
        when_chunk(n, 1, lambda f: h2_begin(1, f))
        when_chunk(n, 2, finish_cross)
        when_chunk(n, 4, finish_local)
        return 0

    lax.fori_loop(0, NC + 4, step, 0)
    grads_last()

    for d in others:
        for h in (0, 1):
            g1_copy(h, d).wait_send()
            g2_copy(h, d).wait_send()
        g3_copy(d).wait_send()

    def drain(f, _):
        cross_copy(f).wait_send()
        for d in range(N):
            local_copy(f, d).wait_send()

        for k in range(N):

            @pl.when(o < 3)
            def _():
                cross_pass(f, k).wait_send()

            @pl.when(k < z)
            def _():
                z_copy(f, k, 1).wait_send()

            @pl.when(k > z)
            def _():
                z_copy(f, k, 0).wait_send()

        for d in others:
            h1_copy(0, f, d).wait_send()
            h1_copy(1, f, d).wait_send()
            h2_copy(f, d).wait_send()
        for r in (0, 1):
            emit(r, f, ahead_out).wait()
        return 0

    lax.fori_loop(0, NC, drain, 0)


def route(routed, pick1, pick2, grads):
    bf16, f32 = jnp.bfloat16, jnp.float32
    vmem, dma = pltpu.VMEM, pltpu.SemaphoreType.DMA
    scratch = [
        vmem((NC, N, ROWS, CW), bf16),
        vmem((NC, N, ROWS, CW), bf16),
        vmem((2, NC, 3, PAIR, CW), bf16),
        vmem((2, NC, N, PAIR, CW), bf16),
        vmem((2, NC, N, ROWS, CW), bf16),
        vmem((NC, 3, ROWS, CW), bf16),
        vmem((NC, 2, 3, ROWS, CW), bf16),
        vmem((2, NC, ROWS, CW), bf16),
        vmem((2, N * PAIR, N * ROWS), bf16),
        vmem((2, N * ROWS, N * PAIR), bf16),
        vmem((2, 3, 128, LANE), bf16),
        vmem((2, 128, LANE), f32),
        vmem((2, 3, 32, LANE), f32),
        vmem((3, 16, LANE), f32),
        vmem((64, LANE), f32),
        dma((NC, N)), dma((NC, N)),
        dma((NC,)), dma((NC, N)), dma((NC, N)),
        dma((2, NC, 3)), dma((2, NC, 3)),
        dma((NC, 3)), dma((NC, 3)),
        dma((NC, N)), dma((NC, 2, 3)),
        dma((2, NC)),
        dma((3, 2, 3)), dma((3, 2, 3)),
    ]
    return pl.pallas_call(
        route_kernel,
        out_shape=(
            jax.ShapeDtypeStruct((ROWS, D), bf16),
            jax.ShapeDtypeStruct((ROWS, D), bf16),
            jax.ShapeDtypeStruct((16, LANE), f32),
        ),
        in_specs=[pl.BlockSpec(memory_space=pltpu.VMEM)] * 4,
        out_specs=(
            pl.BlockSpec(memory_space=pl.ANY),
            pl.BlockSpec(memory_space=pl.ANY),
            pl.BlockSpec(memory_space=pltpu.VMEM),
        ),
        scratch_shapes=scratch,
        compiler_params=pltpu.CompilerParams(
            collective_id=1, has_side_effects=True, vmem_limit_bytes=60 * MIB
        ),
        name="route",
    )(routed, pick1, pick2, grads)


def pool_order(halves):
    rest = halves.shape[2:]
    first = halves[0].reshape((N, N, 2) + rest)
    second = jnp.swapaxes(halves[1].reshape((N, N, 2) + rest), 0, 1)
    return jnp.concatenate([first, second], axis=2).reshape((R,) + rest)


def picks(tables, crossing, flip):
    me = Place()
    grid = tables.reshape(N, N, N, SLOTS)
    coord = jnp.arange(N, dtype=jnp.int32)
    same = coord[:, None] == coord[None, :]
    slot = jnp.arange(SLOTS, dtype=jnp.int32)
    if crossing:
        group = grid[me.x, me.y]
        to = jnp.arange(N * N, dtype=jnp.int32) * 4 + me.z + 1
        mine = me.x * 16 + coord * 4 + me.z + 1
        place = jnp.where(flip, 3 - coord, coord)
        hit = (group[None] == to[:, None, None])[:, :, None, :]
        first = hit & (place[:, None] == coord[None, :])[None, :, :, None]
    else:
        group = grid[:, me.y, me.z]
        to = me.x * 16 + jnp.arange(N * N, dtype=jnp.int32).reshape(N, 1, N) + 1
        mine = me.x * 16 + me.y * 4 + coord + 1
        hit = group[None, :, None, :] == to[..., None]
        first = hit[:, :, :, None, :] & same[None, :, None, :, None]
    sent = jnp.any(tables[None] == mine[:, None, None], axis=2)
    spot = jnp.cumsum(sent.astype(jnp.int32), axis=1) - 1
    spot = jnp.where(sent, spot, -1).reshape(N, N, N, N)
    if crossing:
        spot = lax.dynamic_index_in_dim(spot, me.y, 2, keepdims=False)
        second = (spot[:, None, :, None, :] == slot[None, :, None, None, None]) & same[:, None, None, :, None]
    else:
        spot = lax.dynamic_index_in_dim(spot, me.z, 3, keepdims=False)
        spot = jnp.swapaxes(spot, 1, 2)
        second = (spot[:, None, :, :, None] == slot[None, :, None, None, None]) & same[:, None, None, None, :]
    return (
        first.reshape(N * N * N, N * SLOTS).astype(jnp.bfloat16),
        second.reshape(N * SLOTS, N * N * N).astype(jnp.bfloat16),
    )


def shards(
    activations, cotangents, token_counts, route_ahead, route_back, down_rows, up_rows, norm_gain
):
    sizes = token_counts[0, 0, :SLOTS]
    live = sizes > 0
    entry = jnp.stack(
        [jnp.where(live, route_ahead[0, 0, :SLOTS] + 1, 0), jnp.where(live, route_back[0, 0, :SLOTS] + 1, 0)]
    ).astype(jnp.bfloat16)
    table = jnp.pad(entry[:, None, :], ((0, 0), (0, 15), (0, 128 - SLOTS))).reshape(32, 128)
    own = jnp.concatenate([down_rows[0, 0].reshape(8, LANE), up_rows[0, 0].reshape(8, LANE)], axis=0)
    full, tables = gather(own, table)
    full = full.reshape(R, 16, LANE)
    down_full, up_full = full[:, :8].reshape(R, D), full[:, 8:].reshape(R, D)
    section = lax.axis_index("section")
    tables = pool_order(tables[:, :, ::16, :SLOTS].astype(jnp.int32))
    from_prev = jnp.where(section > 0, tables[:, 0], 0)
    from_next = jnp.where(section < lax.axis_size("section") - 1, tables[:, 1], 0)

    rows = activations.reshape(-1, D)
    grads = cotangents.reshape(-1, D)
    keep = (jnp.arange(TOK, dtype=jnp.int32)[None, :] < sizes[:, None]).astype(jnp.float32).reshape(ROWS, 1)
    routed, grad_down, grad_up = adapter(rows, grads, keep, down_full, up_full, norm_gain)

    odd = section % 2 == 1
    local, cross = jnp.where(odd, from_prev, from_next), jnp.where(odd, from_next, from_prev)
    local1, local2 = picks(local, False, False)
    cross1, cross2 = picks(cross, True, odd)
    share = jnp.concatenate([grad_down.reshape(R, 8, LANE), grad_up.reshape(R, 8, LANE)], axis=1)
    ahead, behind, sums = route(
        routed, jnp.stack([local1, cross1]), jnp.stack([local2, cross2]), share.reshape(R * 16, LANE)
    )
    shape = (1, 1, SLOTS, TOK, D)
    sums = sums.reshape(2, 1, 1, D)
    return (ahead.reshape(shape), behind.reshape(shape), sums[0], sums[1])


def solution(mesh):
    placed = (
        P("section", "pool", None, None, None),
        P("section", "pool", None, None, None),
        P("section", "pool", None),
        P("section", "pool", None),
        P("section", "pool", None),
        P("section", "pool", None),
        P("section", "pool", None),
        P("section", None),
    )
    return jax.shard_map(
        shards,
        mesh=mesh,
        in_specs=placed,
        out_specs=(
            P("section", "pool", None, None, None),
            P("section", "pool", None, None, None),
            P("section", "pool", None),
            P("section", "pool", None),
        ),
        check_vma=False,
    )
```

```python
import functools

import jax
import jax.numpy as jnp
from jax import lax
from jax.experimental import pallas as pl
from jax.experimental.pallas import tpu as pltpu
from jax.sharding import PartitionSpec as P

SLOTS = 12
TOK = 8
ROWS = SLOTS * TOK
N = 4
D = 5120
R = 64
NC = 10
CW = D // NC
LANE = 640
epsilon = 1e-05
MIB = 1 << 20


class Place:
    def __init__(self):
        section = lax.axis_index("section")
        pool = lax.axis_index("pool")
        self.section, self.pool = section, pool
        self.block, self.core = section // 2, section % 2
        self.x, self.y, self.z = pool // 16, (pool // 4) % 4, pool % 4

    def in_block(self, dx=0, dy=0, dz=0):
        x, y, z = (self.x + dx) % N, (self.y + dy) % N, (self.z + dz) % N
        return {"section": self.section, "pool": x * 16 + y * 4 + z}

    def along_z(self, step):
        far = (self.block * N + self.z + step + 4 * N) % (4 * N)
        return {"section": (far // N) * 2 + self.core, "pool": self.pool - self.z + far % N}


def greet(peers):
    barrier = pltpu.get_barrier_semaphore()
    for peer in peers:
        pl.semaphore_signal(barrier, inc=1, device_id=peer, device_id_type=pl.DeviceIdType.MESH)
    pl.semaphore_wait(barrier, len(peers))


def remote(src, dst, send, recv, peer):
    return pltpu.make_async_remote_copy(
        src_ref=src, dst_ref=dst, send_sem=send, recv_sem=recv, device_id=peer, device_id_type=pl.DeviceIdType.MESH
    )


def gather_kernel(own_ref, table_ref, full_ref, tables_ref, tin, both, local_sems, tin_send, tin_recv, send_sems, recv_sems):
    me = Place()
    x, y, z = me.x, me.y, me.z
    others = (1, 2, 3)
    to_next = {"section": (me.section + 1) % 8, "pool": me.pool}
    to_prev = {"section": (me.section + 7) % 8, "pool": me.pool}
    along = {
        "x": {d: me.in_block(dx=d) for d in others},
        "y": {d: me.in_block(dy=d) for d in others},
        "z": {d: me.in_block(dz=d) for d in others},
    }
    greet([to_next, to_prev] + [along[axis][d] for axis in "xyz" for d in others])

    crossing = [
        remote(table_ref.at[pl.ds(0, 16)], tin.at[pl.ds(0, 16)], tin_send.at[0], tin_recv.at[0], to_next),
        remote(table_ref.at[pl.ds(16, 16)], tin.at[pl.ds(16, 16)], tin_send.at[1], tin_recv.at[1], to_prev),
    ]
    for copy in crossing:
        copy.start()

    half, k = z // 2, z % 2
    place = jnp.where(half == 0, x * 8 + y * 2, y * 8 + x * 2)
    started = []

    def spread(a, own, full):
        for d in others:
            copy = remote(own, full.at[half, place + k], send_sems.at[a, d], recv_sems.at[a, z], along["z"][d])
            copy.start()
            started.append(copy)
        local = pltpu.make_async_copy(own, full.at[half, place + k], local_sems.at[a])
        local.start()
        local.wait()

    def collect(a, own, full):
        for d in others:
            origin = (z + d) % N
            h, kk = origin // 2, origin % 2
            here = jnp.where(h == 0, x * 8 + y * 2, y * 8 + x * 2) + kk
            remote(own, full.at[h, here], send_sems.at[a, d], recv_sems.at[a, origin], along["z"][d]).wait_recv()

    def stage(a, full, n, wait):
        for h in (0, 1):
            first, second = ((y, x), (x, y))[h]
            axis = ("yx", "xy")[h][n]
            for d in others:
                size = 2 if n == 0 else 8
                at = (second * 8 + first * 2) if n == 0 else second * 8
                sem = 4 + h * 6 + n * 3 + d - 1
                if wait:
                    at = (second * 8 + ((first - d + N) % N) * 2) if n == 0 else ((second - d + N) % N) * 8
                view = full.at[h, pl.ds(at, size)]
                copy = remote(view, view, send_sems.at[a, sem], recv_sems.at[a, sem], along[axis][d])
                if wait:
                    copy.wait_recv()
                else:
                    copy.start()
                    started.append(copy)

    weights = (0, own_ref, full_ref)
    marks = (1, both, tables_ref)
    spread(*weights)
    for copy in crossing:
        copy.wait_recv()
    both[...] = tin[:16] + tin[16:]
    spread(*marks)
    collect(*weights)
    stage(0, full_ref, 0, False)
    collect(*marks)
    stage(1, tables_ref, 0, False)
    stage(0, full_ref, 0, True)
    stage(0, full_ref, 1, False)
    stage(1, tables_ref, 0, True)
    stage(1, tables_ref, 1, False)
    stage(0, full_ref, 1, True)
    stage(1, tables_ref, 1, True)
    for copy in crossing + started:
        copy.wait_send()


def gather(own, table):
    dma = pltpu.SemaphoreType.DMA
    return pl.pallas_call(
        gather_kernel,
        out_shape=(
            jax.ShapeDtypeStruct((2, R // 2, 16, LANE), jnp.bfloat16),
            jax.ShapeDtypeStruct((2, R // 2, 16, 128), jnp.bfloat16),
        ),
        in_specs=[pl.BlockSpec(memory_space=pltpu.VMEM)] * 2,
        out_specs=(pl.BlockSpec(memory_space=pltpu.VMEM),) * 2,
        scratch_shapes=[
            pltpu.VMEM((32, 128), jnp.bfloat16), pltpu.VMEM((16, 128), jnp.bfloat16),
            dma((2,)), dma((2,)), dma((2,)), dma((2, 16)), dma((2, 16)),
        ],
        compiler_params=pltpu.CompilerParams(
            collective_id=0, has_side_effects=True, vmem_limit_bytes=16 * MIB
        ),
        name="gather",
    )(own, table)


def adapter_kernel(x_ref, g_ref, keep_ref, down_ref, up_ref, gain_ref, routed_ref, gd_ref, gu_ref, normed, through):
    keep = keep_ref[...] > 0.0
    square = jnp.zeros((ROWS, 1), jnp.float32)
    for f in range(NC):
        wide = x_ref[:, f * CW : (f + 1) * CW].astype(jnp.float32)
        square += jnp.sum(wide * wide, axis=1, keepdims=True)
    inv_rms = lax.rsqrt(square * (1.0 / D) + epsilon)
    across = (((1,), (1,)), ((), ()))
    preact = jnp.zeros((ROWS, R), jnp.float32)
    back = jnp.zeros((ROWS, R), jnp.float32)
    for f in range(NC):
        cols = slice(f * CW, (f + 1) * CW)
        wide = x_ref[:, cols].astype(jnp.float32)
        part = (wide * inv_rms * gain_ref[:, cols].astype(jnp.float32)).astype(jnp.bfloat16)
        normed[:, cols] = part
        preact += lax.dot_general(part, down_ref[:, cols], across, preferred_element_type=jnp.float32)
        grad = jnp.where(keep, g_ref[:, cols].astype(jnp.float32), 0.0).astype(jnp.bfloat16)
        back += lax.dot_general(grad, up_ref[:, cols], across, preferred_element_type=jnp.float32)
    gates = jax.nn.sigmoid(preact)
    hidden_wide = (preact * gates).astype(jnp.bfloat16).astype(jnp.float32)
    slope_wide = (back * gates * (1.0 + preact * (1.0 - gates))).astype(jnp.bfloat16).astype(jnp.float32)
    hidden, slope = hidden_wide.astype(jnp.bfloat16), slope_wide.astype(jnp.bfloat16)
    hidden_t, slope_t = hidden_wide.T.astype(jnp.bfloat16), slope_wide.T.astype(jnp.bfloat16)
    centred = jnp.zeros((ROWS, 1), jnp.float32)
    for f in range(NC):
        cols = slice(f * CW, (f + 1) * CW)
        wide = x_ref[:, cols].astype(jnp.float32)
        branch = jnp.dot(hidden, up_ref[:, cols], preferred_element_type=jnp.float32)
        routed_ref[0, f] = jnp.where(keep, wide + branch, 0.0).astype(jnp.bfloat16)
        grad = jnp.where(keep, g_ref[:, cols].astype(jnp.float32), 0.0).astype(jnp.bfloat16)
        gu_ref[:, cols] = jnp.dot(hidden_t, grad, preferred_element_type=jnp.float32).astype(jnp.bfloat16)
        gd_ref[:, cols] = jnp.dot(slope_t, normed[:, cols], preferred_element_type=jnp.float32).astype(jnp.bfloat16)
        part = jnp.dot(slope, down_ref[:, cols], preferred_element_type=jnp.float32)
        part = part * gain_ref[:, cols].astype(jnp.float32)
        through[:, cols] = part
        centred += jnp.sum(part * wide, axis=1, keepdims=True)
    centred = centred * (1.0 / D)
    for f in range(NC):
        cols = slice(f * CW, (f + 1) * CW)
        wide = x_ref[:, cols].astype(jnp.float32)
        grad = jnp.where(keep, g_ref[:, cols].astype(jnp.float32), 0.0)
        inward = grad + inv_rms * (through[:, cols] - wide * inv_rms * inv_rms * centred)
        routed_ref[1, f] = inward.astype(jnp.bfloat16)


def adapter(rows, grads, keep, down_full, up_full, gain_row):
    whole = lambda shape: pl.BlockSpec(shape, lambda i: (0,) * len(shape))
    return pl.pallas_call(
        adapter_kernel,
        grid=(1,),
        out_shape=(
            jax.ShapeDtypeStruct((2, NC, ROWS, CW), jnp.bfloat16),
            jax.ShapeDtypeStruct((R, D), jnp.bfloat16),
            jax.ShapeDtypeStruct((R, D), jnp.bfloat16),
        ),
        in_specs=[
            whole((ROWS, D)),
            whole((ROWS, D)),
            whole((ROWS, 1)),
            whole((R, D)),
            whole((R, D)),
            whole((1, D)),
        ],
        out_specs=(whole((2, NC, ROWS, CW)), whole((R, D)), whole((R, D))),
        scratch_shapes=[pltpu.VMEM((ROWS, D), jnp.bfloat16), pltpu.VMEM((ROWS, D), jnp.float32)],
        compiler_params=pltpu.CompilerParams(vmem_limit_bytes=40 * MIB),
        cost_estimate=pl.CostEstimate(flops=6 * 2 * ROWS * R * D, bytes_accessed=10 * MIB, transcendentals=ROWS * R),
        name="adapter",
    )(rows, grads, keep, down_full, up_full, gain_row)


def repeat_matrix(rows, cols, times, along):
    r = lax.broadcasted_iota(jnp.int32, (rows, cols), 0)
    c = lax.broadcasted_iota(jnp.int32, (rows, cols), 1)
    return ((r // times == c) if along == 0 else (c // times == r)).astype(jnp.bfloat16)


def spread_tokens(small):
    a, b = small.shape
    tall = jnp.dot(repeat_matrix(TOK * a, a, TOK, 0), small, preferred_element_type=jnp.float32).astype(jnp.bfloat16)
    wide = jnp.dot(tall, repeat_matrix(b, TOK * b, TOK, 1), preferred_element_type=jnp.float32)
    r = lax.broadcasted_iota(jnp.int32, (TOK * a, TOK * b), 0) % TOK
    c = lax.broadcasted_iota(jnp.int32, (TOK * a, TOK * b), 1) % TOK
    return jnp.where(r == c, wide, 0.0).astype(jnp.bfloat16)


PAIR = N * N * TOK
PLAN = (
    ("cross_start", -2),
    ("local_start", -3),
    ("cross_pass", 0),
    ("merge_first", 4),
    ("merge_second", 6),
    ("local_pick", 0),
    ("cross_pick", 1),
    ("local_sort", 2),
    ("grads", 0),
    ("cross_sort", 3),
    ("cross_end", 5),
    ("local_end", 8),
)
GRADS = (5, 7, 9)


def route_kernel(
    src, local1, local2, cross1, cross2, grads,
    ahead_out, behind_out, down_out, up_out,
    lbuf, dbuf, h1s, h1r, h2s, last, zpart, result, m1, m2,
    g1, g1_sum, g2, g3, total,
    sent, lrecv, drecv, h1recv, h2recv, zrecv, out_sem,
    gsend, grecv,
):
    me = Place()
    x, y, z, core = me.x, me.y, me.z, me.core
    o = jnp.where(core == 0, z, 3 - z)
    znext = me.along_z(1 - 2 * core)
    others = (1, 2, 3)
    along = {"x": {d: me.in_block(dx=d) for d in others}, "y": {d: me.in_block(dy=d) for d in others}}
    zup, zdown = me.in_block(dz=1), me.in_block(dz=3)
    other_core = me.section + 1 - 2 * core

    def facing(d):
        return {"section": other_core, "pool": ((x + d) % N) * 16 + y * 4 + z}

    entry = {
        "section": ((me.block + 2 * core - 1 + N) % N) * 2 + 1 - core,
        "pool": me.pool - z + 3 * (1 - core),
    }
    so = jnp.where(core == 1, z, 3 - z)

    barrier = pltpu.get_barrier_semaphore()

    def hello(peer):
        pl.semaphore_signal(barrier, inc=1, device_id=peer, device_id_type=pl.DeviceIdType.MESH)

    everyone = [me.in_block(dz=d) for d in others] + [along["x"][d] for d in others] + [along["y"][d] for d in others]
    everyone += [znext, me.along_z(2 * core - 1)]
    everyone += [facing(d) for d in range(N)]
    for way in (1, N - 1):
        for k in range(N):
            everyone.append({"section": ((me.block + way) % N) * 2 + 1 - core, "pool": me.pool - z + k})
    for peer in everyone:
        hello(peer)
    pl.semaphore_wait(barrier, len(everyone))

    def local_copy(f, d):
        return remote(src.at[core, f], lbuf.at[f, x], sent.at[0], lrecv.at[f], facing(d))

    def cross_copy(f):
        return remote(src.at[1 - core, f], dbuf.at[f, so], sent.at[1], drecv.at[f, so], entry)

    def cross_pass(f, k):
        return remote(dbuf.at[f, k], dbuf.at[f, k], sent.at[2], drecv.at[f, k], znext)

    def h1_copy(r, f, d):
        return remote(
            h1s.at[r, f, d - 1], h1r.at[r, f, x if r else y], sent.at[3], h1recv.at[r, f],
            along["x" if r else "y"][d],
        )

    def h2_copy(f, d):
        return remote(h2s.at[1, f, d], last.at[f, d - 1], sent.at[4], h2recv.at[f], along["y"][d])

    def z_copy(f, to, way):
        slot = (z - to - 1) if way else (to - z - 1)
        return remote(
            h2s.at[0, f, to], zpart.at[f, way, slot], sent.at[5], zrecv.at[f, way, slot], zdown if way else zup
        )

    def z_arrival(f, slot, way):
        return remote(
            h2s.at[0, f, 0], zpart.at[f, way, slot], sent.at[5], zrecv.at[f, way, slot], zdown if way else zup
        )

    def arrived(ref, sem):
        remote(ref, ref, sent.at[0], sem, zup).wait_recv()

    def left(ref, n):
        remote(ref, ref, sent.at[n], zrecv.at[0, 0, 0], zup).wait_send()

    def emit(r, f, out):
        cols = pl.ds(pl.multiple_of(f * CW, 128), CW)
        return pltpu.make_async_copy(result.at[r, f], out.at[:, cols], out_sem)

    def local_start(f):
        for d in (2, 1, 3, 0):
            local_copy(f, d).start()

    def pass_on(f):
        for k in (3, 2, 1, 0):
            cross_pass(f, k).wait_recv()

            @pl.when(o < 3)
            def _():
                cross_pass(f, k).start()

    def h1_begin(r, f):
        if r == 0:
            arrived(lbuf.at[f], lrecv.at[f])
        here = x if r else y
        block = (dbuf if r else lbuf)[f].reshape(N * ROWS, CW)
        for d in (2, 1, 3, 0):
            to = (here + d) % N
            pick = m1[r, pl.ds(pl.multiple_of(to * PAIR, PAIR), PAIR), :]
            rows = jnp.dot(pick, block, preferred_element_type=jnp.float32).astype(jnp.bfloat16)
            if d == 0:
                h1r[r, f, here] = rows
            else:
                h1s[r, f, d - 1] = rows
                h1_copy(r, f, d).start()

    def h2_begin(r, f):
        arrived(h1s.at[r, f], h1recv.at[r, f])
        block = h1r[r, f].reshape(N * PAIR, CW)
        for d in (2, 1, 3, 0):
            to = (y + d) % N if r else d
            pick = m2[r, pl.ds(pl.multiple_of(to * ROWS, ROWS), ROWS), :]
            h2s[r, f, d] = jnp.dot(pick, block, preferred_element_type=jnp.float32).astype(jnp.bfloat16)
            if r and d:
                h2_copy(f, d).start()
        if r == 0:

            @pl.when(z == 0)
            def _():
                for to in (3, 2, 1):
                    z_copy(f, to, 0).start()

            @pl.when(z == 3)
            def _():
                for to in (0, 1, 2):
                    z_copy(f, to, 1).start()

    def add_on(f, to, way):
        slot = (z - to) if way else (to - z)
        z_arrival(f, slot, way).wait_recv()
        h2s[0, f, to] = h2s[0, f, to] + zpart[f, way, slot]
        z_copy(f, to, way).start()

    def merge_first(f):
        @pl.when(z == 1)
        def _():
            add_on(f, 3, 0)
            add_on(f, 2, 0)

        @pl.when(z == 2)
        def _():
            add_on(f, 0, 1)
            add_on(f, 1, 1)

    def merge_second(f):
        @pl.when(z == 2)
        def _():
            add_on(f, 3, 0)

        @pl.when(z == 1)
        def _():
            add_on(f, 0, 1)

    def hand_out(r, f):
        @pl.when(core == 1 - r)
        def _():
            emit(r, f, ahead_out).start()

        @pl.when(core == r)
        def _():
            emit(r, f, behind_out).start()

    def finish_local(f):
        result[0, f] = h2s[0, f, z]

        @pl.when(z > 0)
        def _():
            z_arrival(f, 0, 0).wait_recv()
            result[0, f] = result[0, f] + zpart[f, 0, 0]

        @pl.when(z < 3)
        def _():
            z_arrival(f, 0, 1).wait_recv()
            result[0, f] = result[0, f] + zpart[f, 1, 0]

        hand_out(0, f)

    def finish_cross(f):
        arrived(last.at[f], h2recv.at[f])
        result[1, f] = (h2s[1, f, 0] + last[f, 0]) + (last[f, 1] + last[f, 2])
        hand_out(1, f)

    G1, G2, G3 = 128, 32, 16

    def axis_of(n, h):
        return "xy"[(n + h) % 2]

    def at(axis):
        return x if axis == "x" else y

    def g1_copy(h, d):
        axis = axis_of(0, h)
        to = (at(axis) + d) % N
        return remote(
            grads.at[pl.ds(h * 512 + to * G1, G1)], g1.at[h, d - 1], gsend.at[0, h, d - 1], grecv.at[0, h, d - 1],
            along[axis][d],
        )

    def g2_copy(h, d):
        axis = axis_of(1, h)
        to = (at(axis) + d) % N
        return remote(
            g1_sum.at[h, pl.ds(to * G2, G2)], g2.at[h, d - 1], gsend.at[1, h, d - 1], grecv.at[1, h, d - 1],
            along[axis][d],
        )

    def g3_copy(d):
        to = (z + d) % N
        return remote(
            total.at[pl.ds(to * G3, G3)], g3.at[d - 1], gsend.at[2, 0, d - 1], grecv.at[2, 0, d - 1], me.in_block(dz=d)
        )

    def add_three(own, parts):
        return (own + parts[0].astype(jnp.float32)) + (parts[1].astype(jnp.float32) + parts[2].astype(jnp.float32))

    def grads_first():
        for h in (0, 1):
            for d in others:
                g1_copy(h, d).start()

    def grads_second():
        for h in (0, 1):
            for d in others:
                g1_copy(h, d).wait_recv()
            row = pl.multiple_of(h * 512 + at(axis_of(0, h)) * G1, G1)
            g1_sum[h] = add_three(grads[pl.ds(row, G1), :].astype(jnp.float32), g1[h])
            for d in others:
                g2_copy(h, d).start()

    def grads_third():
        for h in (0, 1):
            for d in others:
                g2_copy(h, d).wait_recv()
            row = pl.multiple_of(at(axis_of(1, h)) * G2, G2)
            total[pl.ds(h * G2, G2), :] = add_three(g1_sum[h, pl.ds(row, G2), :], g2[h])
        for d in others:
            g3_copy(d).start()

    def grads_last():
        for d in others:
            g3_copy(d).wait_recv()
        both = add_three(total[pl.ds(pl.multiple_of(z * G3, G3), G3), :], g3[...])
        for j in range(8):
            down_out[:, j * LANE : (j + 1) * LANE] = both[j : j + 1]
            up_out[:, j * LANE : (j + 1) * LANE] = both[8 + j : 9 + j]

    steps = {
        "cross_start": lambda f: cross_copy(f).start(),
        "local_start": local_start,
        "local_pick": lambda f: h1_begin(0, f),
        "merge_first": merge_first,
        "merge_second": merge_second,
        "cross_pass": pass_on,
        "cross_pick": lambda f: h1_begin(1, f),
        "local_sort": lambda f: h2_begin(0, f),
        "cross_sort": lambda f: h2_begin(1, f),
        "cross_end": finish_cross,
        "local_end": finish_local,
    }
    for name, lag in PLAN:
        for f in range(min(-lag, NC)):
            steps[name](f)
    for r, (pick1, pick2) in enumerate(((local1, local2), (cross1, cross2))):
        m1[r] = spread_tokens(pick1[...])
        m2[r] = spread_tokens(pick2[...])

    def turn(n, _):
        for name, lag in PLAN:
            if name == "grads":
                for when, run in zip(GRADS, (grads_first, grads_second, grads_third)):
                    pl.when(n == when)(run)
            elif -lag < NC:
                pl.when((n >= lag) & (n < NC + lag))(functools.partial(steps[name], n - lag))
        return 0

    lax.fori_loop(0, NC + max(lag for _, lag in PLAN), turn, 0)
    grads_last()

    for d in others:
        for h in (0, 1):
            g1_copy(h, d).wait_send()
            g2_copy(h, d).wait_send()
        g3_copy(d).wait_send()

    left(lbuf, 0)
    left(src.at[0], 1)
    pl.when(o < 3)(lambda: left(dbuf, 2))
    left(h1s, 3)
    left(last, 4)
    left(last, 5)
    pltpu.make_async_copy(result, result, out_sem).wait()


def route(routed, local1, local2, cross1, cross2, grads):
    bf16, f32 = jnp.bfloat16, jnp.float32
    vmem, dma = pltpu.VMEM, pltpu.SemaphoreType.DMA
    scratch = [
        vmem((NC, N, ROWS, CW), bf16),
        vmem((NC, N, ROWS, CW), bf16),
        vmem((2, NC, 3, PAIR, CW), bf16),
        vmem((2, NC, N, PAIR, CW), bf16),
        vmem((2, NC, N, ROWS, CW), bf16),
        vmem((NC, 3, ROWS, CW), bf16),
        vmem((NC, 2, 3, ROWS, CW), bf16),
        vmem((2, NC, ROWS, CW), bf16),
        vmem((2, N * PAIR, N * ROWS), bf16),
        vmem((2, N * ROWS, N * PAIR), bf16),
        vmem((2, 3, 128, LANE), bf16),
        vmem((2, 128, LANE), f32),
        vmem((2, 3, 32, LANE), f32),
        vmem((3, 16, LANE), f32),
        vmem((64, LANE), f32),
        dma((6,)),
        dma((NC,)), dma((NC, N)),
        dma((2, NC)), dma((NC,)), dma((NC, 2, 3)),
        dma,
        dma((3, 2, 3)), dma((3, 2, 3)),
    ]
    return pl.pallas_call(
        route_kernel,
        out_shape=(
            jax.ShapeDtypeStruct((ROWS, D), bf16),
            jax.ShapeDtypeStruct((ROWS, D), bf16),
            jax.ShapeDtypeStruct((1, D), f32),
            jax.ShapeDtypeStruct((1, D), f32),
        ),
        in_specs=[pl.BlockSpec(memory_space=pltpu.VMEM)] * 6,
        out_specs=(
            pl.BlockSpec(memory_space=pl.ANY),
            pl.BlockSpec(memory_space=pl.ANY),
            pl.BlockSpec(memory_space=pltpu.VMEM),
            pl.BlockSpec(memory_space=pltpu.VMEM),
        ),
        scratch_shapes=scratch,
        compiler_params=pltpu.CompilerParams(
            collective_id=1, has_side_effects=True, vmem_limit_bytes=60 * MIB
        ),
        name="route",
    )(routed, local1, local2, cross1, cross2, grads)


def pool_order(halves):
    rest = halves.shape[2:]
    first = halves[0].reshape((N, N, 2) + rest)
    second = jnp.swapaxes(halves[1].reshape((N, N, 2) + rest), 0, 1)
    return jnp.concatenate([first, second], axis=2).reshape((R,) + rest)


def picks(tables, crossing, flip):
    me = Place()
    grid = tables.reshape(N, N, N, SLOTS)
    coord = jnp.arange(N, dtype=jnp.int32)
    same = coord[:, None] == coord[None, :]
    slot = jnp.arange(SLOTS, dtype=jnp.int32)
    if crossing:
        group = grid[me.x, me.y]
        to = jnp.arange(N * N, dtype=jnp.int32) * 4 + me.z + 1
        mine = me.x * 16 + coord * 4 + me.z + 1
        place = jnp.where(flip, 3 - coord, coord)
        hit = (group[None] == to[:, None, None])[:, :, None, :]
        first = hit & (place[:, None] == coord[None, :])[None, :, :, None]
    else:
        group = grid[:, me.y, me.z]
        to = me.x * 16 + jnp.arange(N * N, dtype=jnp.int32).reshape(N, 1, N) + 1
        mine = me.x * 16 + me.y * 4 + coord + 1
        hit = group[None, :, None, :] == to[..., None]
        first = hit[:, :, :, None, :] & same[None, :, None, :, None]
    sent = jnp.any(tables[None] == mine[:, None, None], axis=2)
    spot = jnp.cumsum(sent.astype(jnp.int32), axis=1) - 1
    spot = jnp.where(sent, spot, -1).reshape(N, N, N, N)
    if crossing:
        spot = lax.dynamic_index_in_dim(spot, me.y, 2, keepdims=False)
        second = (spot[:, None, :, None, :] == slot[None, :, None, None, None]) & same[:, None, None, :, None]
    else:
        spot = lax.dynamic_index_in_dim(spot, me.z, 3, keepdims=False)
        spot = jnp.swapaxes(spot, 1, 2)
        second = (spot[:, None, :, :, None] == slot[None, :, None, None, None]) & same[:, None, None, None, :]
    return (
        first.reshape(N * N * N, N * SLOTS).astype(jnp.bfloat16),
        second.reshape(N * SLOTS, N * N * N).astype(jnp.bfloat16),
    )


def shards(
    activations, cotangents, token_counts, route_ahead, route_back, down_rows, up_rows, norm_gain
):
    sizes = token_counts[0, 0, :SLOTS]
    live = sizes > 0
    entry = [jnp.where(live, to[0, 0, :SLOTS] + 1, 0).astype(jnp.bfloat16) for to in (route_ahead, route_back)]
    table = jnp.concatenate(
        [jnp.pad(row[None], ((i, 15 - i), (0, 128 - SLOTS))) for i, row in enumerate(entry)], axis=0
    )
    own = jnp.concatenate([down_rows[0, 0].reshape(8, LANE), up_rows[0, 0].reshape(8, LANE)], axis=0)
    full, tables = gather(own, table)
    full = full.reshape(R, 16, LANE)
    down_full, up_full = full[:, :8].reshape(R, D), full[:, 8:].reshape(R, D)
    section = lax.axis_index("section")
    tables = pool_order(tables[:, :, :2, :SLOTS].astype(jnp.int32))
    from_prev = jnp.where(section > 0, tables[:, 0], 0)
    from_next = jnp.where(section < lax.axis_size("section") - 1, tables[:, 1], 0)

    rows = activations.reshape(-1, D)
    grads = cotangents.reshape(-1, D)
    keep = (jnp.arange(TOK, dtype=jnp.int32)[None, :] < sizes[:, None]).astype(jnp.float32).reshape(ROWS, 1)
    routed, grad_down, grad_up = adapter(rows, grads, keep, down_full, up_full, norm_gain)

    odd = section % 2 == 1
    local, cross = jnp.where(odd, from_prev, from_next), jnp.where(odd, from_next, from_prev)
    local1, local2 = picks(local, False, False)
    cross1, cross2 = picks(cross, True, odd)
    share = jnp.concatenate([grad_down.reshape(R, 8, LANE), grad_up.reshape(R, 8, LANE)], axis=1)
    ahead, behind, sum_down, sum_up = route(routed, local1, local2, cross1, cross2, share.reshape(R * 16, LANE))
    shape = (1, 1, SLOTS, TOK, D)
    return (ahead.reshape(shape), behind.reshape(shape), sum_down[None], sum_up[None])


def solution(mesh):
    placed = (
        P("section", "pool", None, None, None),
        P("section", "pool", None, None, None),
        P("section", "pool", None),
        P("section", "pool", None),
        P("section", "pool", None),
        P("section", "pool", None),
        P("section", "pool", None),
        P("section", None),
    )
    return jax.shard_map(
        shards,
        mesh=mesh,
        in_specs=placed,
        out_specs=(
            P("section", "pool", None, None, None),
            P("section", "pool", None, None, None),
            P("section", "pool", None),
            P("section", "pool", None),
        ),
        check_vma=False,
    )
```

```python
import functools

import jax
import jax.numpy as jnp
from jax import lax
from jax.experimental import pallas as pl
from jax.experimental.pallas import tpu as pltpu
from jax.sharding import PartitionSpec as P

SLOTS = 12
TOK = 8
ROWS = SLOTS * TOK
N = 4
D = 5120
R = 64
NC = 10
CW = D // NC
LANE = 640
epsilon = 1e-05
MIB = 1 << 20


class Place:
    def __init__(self):
        section = lax.axis_index("section")
        pool = lax.axis_index("pool")
        self.section, self.pool = section, pool
        self.block, self.core = section // 2, section % 2
        self.x, self.y, self.z = pool // 16, (pool // 4) % 4, pool % 4

    def in_block(self, dx=0, dy=0, dz=0):
        x, y, z = (self.x + dx) % N, (self.y + dy) % N, (self.z + dz) % N
        return {"section": self.section, "pool": x * 16 + y * 4 + z}

    def along_z(self, step):
        far = (self.block * N + self.z + step + 4 * N) % (4 * N)
        return {"section": (far // N) * 2 + self.core, "pool": self.pool - self.z + far % N}


def greet(peers):
    barrier = pltpu.get_barrier_semaphore()
    for peer in peers:
        pl.semaphore_signal(barrier, inc=1, device_id=peer, device_id_type=pl.DeviceIdType.MESH)
    pl.semaphore_wait(barrier, len(peers))


def remote(src, dst, send, recv, peer):
    return pltpu.make_async_remote_copy(
        src_ref=src, dst_ref=dst, send_sem=send, recv_sem=recv, device_id=peer, device_id_type=pl.DeviceIdType.MESH
    )


def gather_kernel(own_ref, table_ref, full_ref, tables_ref, tin, both, tin_send, tin_recv, send_sems, recv_sems):
    me = Place()
    x, y, z = me.x, me.y, me.z
    others = (1, 2, 3)
    to_next = {"section": (me.section + 1) % 8, "pool": me.pool}
    to_prev = {"section": (me.section + 7) % 8, "pool": me.pool}
    along = {
        "x": {d: me.in_block(dx=d) for d in others},
        "y": {d: me.in_block(dy=d) for d in others},
        "z": {d: me.in_block(dz=d) for d in others},
    }
    greet([to_next, to_prev] + [along[axis][d] for axis in "xyz" for d in others])

    crossing = [
        remote(table_ref.at[pl.ds(0, 16)], tin.at[pl.ds(0, 16)], tin_send.at[0], tin_recv.at[0], to_next),
        remote(table_ref.at[pl.ds(16, 16)], tin.at[pl.ds(16, 16)], tin_send.at[1], tin_recv.at[1], to_prev),
    ]
    for copy in crossing:
        copy.start()

    half, k = z // 2, z % 2
    place = jnp.where(half == 0, x * 8 + y * 2, y * 8 + x * 2)

    def spread(a, own, full):
        for d in others:
            remote(own, full.at[half, place + k], send_sems.at[a, 0], recv_sems.at[a, 0], along["z"][d]).start()
        full[half, place + k] = own[...]

    def group(a, full, n, size, h, wait):
        view = full.at[h, pl.ds(0, 3 * size)]
        sem = 0 if n < 0 else 1 + 2 * n + h
        copy = remote(view, view, send_sems.at[a, sem], recv_sems.at[a, sem], along["z"][1])
        copy.wait_recv() if wait else copy.wait_send()

    def collect(a, own, full):
        group(a, full, -1, 1, 0, True)

    def stage(a, full, n, wait):
        size = (2, 8)[n]
        for h in (0, 1):
            first, second = ((y, x), (x, y))[h]
            axis = ("yx", "xy")[h][n]
            at = (second * 8 + first * 2) if n == 0 else second * 8
            if wait:
                group(a, full, n, size, h, True)
                continue
            for d in (2, 1, 3):
                view = full.at[h, pl.ds(at, size)]
                sem = 1 + 2 * n + h
                remote(view, view, send_sems.at[a, sem], recv_sems.at[a, sem], along[axis][d]).start()

    weights = (0, own_ref, full_ref)
    marks = (1, both, tables_ref)
    spread(*weights)
    for copy in crossing:
        copy.wait_recv()
    both[...] = tin[:16] + tin[16:]
    spread(*marks)
    collect(*weights)
    stage(0, full_ref, 0, False)
    collect(*marks)
    stage(1, tables_ref, 0, False)
    stage(0, full_ref, 0, True)
    stage(0, full_ref, 1, False)
    stage(1, tables_ref, 0, True)
    stage(1, tables_ref, 1, False)
    stage(0, full_ref, 1, True)
    stage(1, tables_ref, 1, True)
    for copy in crossing:
        copy.wait_send()
    for a, full in ((0, full_ref), (1, tables_ref)):
        group(a, full, -1, 1, 0, False)
        for n, size in ((0, 2), (1, 8)):
            for h in (0, 1):
                group(a, full, n, size, h, False)


def gather(own, table):
    dma = pltpu.SemaphoreType.DMA
    return pl.pallas_call(
        gather_kernel,
        out_shape=(
            jax.ShapeDtypeStruct((2, R // 2, 16, LANE), jnp.bfloat16),
            jax.ShapeDtypeStruct((2, R // 2, 16, 128), jnp.bfloat16),
        ),
        in_specs=[pl.BlockSpec(memory_space=pltpu.VMEM)] * 2,
        out_specs=(pl.BlockSpec(memory_space=pltpu.VMEM),) * 2,
        scratch_shapes=[
            pltpu.VMEM((32, 128), jnp.bfloat16), pltpu.VMEM((16, 128), jnp.bfloat16),
            dma((2,)), dma((2,)), dma((2, 5)), dma((2, 5)),
        ],
        compiler_params=pltpu.CompilerParams(
            collective_id=0, has_side_effects=True, vmem_limit_bytes=16 * MIB
        ),
        name="gather",
    )(own, table)


def adapter_kernel(x_ref, g_ref, keep_ref, down_ref, up_ref, gain_ref, routed_ref, gd_ref, gu_ref, normed, through):
    keep = keep_ref[...] > 0.0
    square = jnp.zeros((ROWS, 1), jnp.float32)
    for f in range(NC):
        wide = x_ref[:, f * CW : (f + 1) * CW].astype(jnp.float32)
        square += jnp.sum(wide * wide, axis=1, keepdims=True)
    inv_rms = lax.rsqrt(square * (1.0 / D) + epsilon)
    across = (((1,), (1,)), ((), ()))
    preact = jnp.zeros((ROWS, R), jnp.float32)
    back = jnp.zeros((ROWS, R), jnp.float32)
    for f in range(NC):
        cols = slice(f * CW, (f + 1) * CW)
        wide = x_ref[:, cols].astype(jnp.float32)
        part = (wide * inv_rms * gain_ref[:, cols].astype(jnp.float32)).astype(jnp.bfloat16)
        normed[:, cols] = part
        preact += lax.dot_general(part, down_ref[:, cols], across, preferred_element_type=jnp.float32)
        grad = jnp.where(keep, g_ref[:, cols].astype(jnp.float32), 0.0).astype(jnp.bfloat16)
        back += lax.dot_general(grad, up_ref[:, cols], across, preferred_element_type=jnp.float32)
    gates = jax.nn.sigmoid(preact)
    hidden_wide = (preact * gates).astype(jnp.bfloat16).astype(jnp.float32)
    slope_wide = (back * gates * (1.0 + preact * (1.0 - gates))).astype(jnp.bfloat16).astype(jnp.float32)
    hidden, slope = hidden_wide.astype(jnp.bfloat16), slope_wide.astype(jnp.bfloat16)
    hidden_t, slope_t = hidden_wide.T.astype(jnp.bfloat16), slope_wide.T.astype(jnp.bfloat16)
    centred = jnp.zeros((ROWS, 1), jnp.float32)
    for f in range(NC):
        cols = slice(f * CW, (f + 1) * CW)
        wide = x_ref[:, cols].astype(jnp.float32)
        branch = jnp.dot(hidden, up_ref[:, cols], preferred_element_type=jnp.float32)
        routed_ref[0, f] = jnp.where(keep, wide + branch, 0.0).astype(jnp.bfloat16)
        grad = jnp.where(keep, g_ref[:, cols].astype(jnp.float32), 0.0).astype(jnp.bfloat16)
        gu_ref[:, cols] = jnp.dot(hidden_t, grad, preferred_element_type=jnp.float32).astype(jnp.bfloat16)
        gd_ref[:, cols] = jnp.dot(slope_t, normed[:, cols], preferred_element_type=jnp.float32).astype(jnp.bfloat16)
        part = jnp.dot(slope, down_ref[:, cols], preferred_element_type=jnp.float32)
        part = part * gain_ref[:, cols].astype(jnp.float32)
        through[:, cols] = part
        centred += jnp.sum(part * wide, axis=1, keepdims=True)
    centred = centred * (1.0 / D)
    for f in range(NC):
        cols = slice(f * CW, (f + 1) * CW)
        wide = x_ref[:, cols].astype(jnp.float32)
        grad = jnp.where(keep, g_ref[:, cols].astype(jnp.float32), 0.0)
        inward = grad + inv_rms * (through[:, cols] - wide * inv_rms * inv_rms * centred)
        routed_ref[1, f] = inward.astype(jnp.bfloat16)


def adapter(rows, grads, keep, down_full, up_full, gain_row):
    whole = lambda shape: pl.BlockSpec(shape, lambda i: (0,) * len(shape))
    return pl.pallas_call(
        adapter_kernel,
        grid=(1,),
        out_shape=(
            jax.ShapeDtypeStruct((2, NC, ROWS, CW), jnp.bfloat16),
            jax.ShapeDtypeStruct((R, D), jnp.bfloat16),
            jax.ShapeDtypeStruct((R, D), jnp.bfloat16),
        ),
        in_specs=[
            whole((ROWS, D)),
            whole((ROWS, D)),
            whole((ROWS, 1)),
            whole((R, D)),
            whole((R, D)),
            whole((1, D)),
        ],
        out_specs=(whole((2, NC, ROWS, CW)), whole((R, D)), whole((R, D))),
        scratch_shapes=[pltpu.VMEM((ROWS, D), jnp.bfloat16), pltpu.VMEM((ROWS, D), jnp.float32)],
        compiler_params=pltpu.CompilerParams(vmem_limit_bytes=40 * MIB),
        cost_estimate=pl.CostEstimate(flops=6 * 2 * ROWS * R * D, bytes_accessed=10 * MIB, transcendentals=ROWS * R),
        name="adapter",
    )(rows, grads, keep, down_full, up_full, gain_row)


def repeat_matrix(rows, cols, times, along):
    r = lax.broadcasted_iota(jnp.int32, (rows, cols), 0)
    c = lax.broadcasted_iota(jnp.int32, (rows, cols), 1)
    return ((r // times == c) if along == 0 else (c // times == r)).astype(jnp.bfloat16)


def spread_tokens(small):
    a, b = small.shape
    tall = jnp.dot(repeat_matrix(TOK * a, a, TOK, 0), small, preferred_element_type=jnp.float32).astype(jnp.bfloat16)
    wide = jnp.dot(tall, repeat_matrix(b, TOK * b, TOK, 1), preferred_element_type=jnp.float32)
    r = lax.broadcasted_iota(jnp.int32, (TOK * a, TOK * b), 0) % TOK
    c = lax.broadcasted_iota(jnp.int32, (TOK * a, TOK * b), 1) % TOK
    return jnp.where(r == c, wide, 0.0).astype(jnp.bfloat16)


PAIR = N * N * TOK
PLAN = (
    ("cross_start", -2),
    ("local_start", -3),
    ("cross_pass", 0),
    ("merge_first", 4),
    ("merge_second", 6),
    ("local_pick", 0),
    ("cross_pick", 1),
    ("local_sort", 2),
    ("grads", 0),
    ("cross_sort", 3),
    ("cross_end", 5),
    ("local_end", 8),
)
GRADS = (3, 5, 7)


def route_kernel(
    src, local1, local2, cross1, cross2, grads,
    ahead_out, behind_out, down_out, up_out,
    lbuf, dbuf, h1s, h1r, h2s, last, zpart, result, m1, m2,
    g1, g1_sum, g2, g3, total,
    sent, lrecv, drecv, h1recv, h2recv, zrecv, out_sem,
    gsend, grecv,
):
    me = Place()
    x, y, z, core = me.x, me.y, me.z, me.core
    o = jnp.where(core == 0, z, 3 - z)
    znext = me.along_z(1 - 2 * core)
    others = (1, 2, 3)
    along = {"x": {d: me.in_block(dx=d) for d in others}, "y": {d: me.in_block(dy=d) for d in others}}
    zup, zdown = me.in_block(dz=1), me.in_block(dz=3)
    other_core = me.section + 1 - 2 * core

    def facing(d):
        return {"section": other_core, "pool": ((x + d) % N) * 16 + y * 4 + z}

    entry = {
        "section": ((me.block + 2 * core - 1 + N) % N) * 2 + 1 - core,
        "pool": me.pool - z + 3 * (1 - core),
    }
    so = jnp.where(core == 1, z, 3 - z)

    barrier = pltpu.get_barrier_semaphore()

    def hello(peer):
        pl.semaphore_signal(barrier, inc=1, device_id=peer, device_id_type=pl.DeviceIdType.MESH)

    everyone = [me.in_block(dz=d) for d in others] + [along["x"][d] for d in others] + [along["y"][d] for d in others]
    everyone += [znext, me.along_z(2 * core - 1)]
    everyone += [facing(d) for d in range(N)]
    for way in (1, N - 1):
        for k in range(N):
            everyone.append({"section": ((me.block + way) % N) * 2 + 1 - core, "pool": me.pool - z + k})
    for peer in everyone:
        hello(peer)
    pl.semaphore_wait(barrier, len(everyone))

    def local_copy(f, d):
        return remote(src.at[core, f], lbuf.at[f, x], sent.at[0], lrecv.at[f], facing(d))

    def cross_copy(f):
        return remote(src.at[1 - core, f], dbuf.at[f, so], sent.at[1], drecv.at[f, so], entry)

    def cross_pass(f, k):
        return remote(dbuf.at[f, k], dbuf.at[f, k], sent.at[2], drecv.at[f, k], znext)

    def h1_copy(r, f, d):
        return remote(
            h1s.at[r, f, d - 1], h1r.at[r, f, x if r else y], sent.at[3], h1recv.at[r, f],
            along["x" if r else "y"][d],
        )

    def h2_copy(f, d):
        return remote(h2s.at[1, f, d], last.at[f, d - 1], sent.at[4], h2recv.at[f], along["y"][d])

    def z_copy(f, to, way):
        slot = (z - to - 1) if way else (to - z - 1)
        return remote(
            h2s.at[0, f, to], zpart.at[f, way, slot], sent.at[5], zrecv.at[f, way, slot], zdown if way else zup
        )

    def z_arrival(f, slot, way):
        return remote(
            h2s.at[0, f, 0], zpart.at[f, way, slot], sent.at[5], zrecv.at[f, way, slot], zdown if way else zup
        )

    def arrived(ref, sem):
        remote(ref, ref, sent.at[0], sem, zup).wait_recv()

    def left(ref, n):
        remote(ref, ref, sent.at[n], zrecv.at[0, 0, 0], zup).wait_send()

    def emit(r, f, out):
        cols = pl.ds(pl.multiple_of(f * CW, 128), CW)
        return pltpu.make_async_copy(result.at[r, f], out.at[:, cols], out_sem)

    def local_start(f):
        for d in (2, 1, 3, 0):
            local_copy(f, d).start()

    def pass_on(f):
        for k in (3, 2, 1, 0):
            cross_pass(f, k).wait_recv()

            @pl.when(o < 3)
            def _():
                cross_pass(f, k).start()

    def h1_begin(r, f):
        if r == 0:
            arrived(lbuf.at[f], lrecv.at[f])
        here = x if r else y
        block = (dbuf if r else lbuf)[f].reshape(N * ROWS, CW)
        for d in (2, 1, 3, 0):
            to = (here + d) % N
            pick = m1[r, pl.ds(pl.multiple_of(to * PAIR, PAIR), PAIR), :]
            rows = jnp.dot(pick, block, preferred_element_type=jnp.float32).astype(jnp.bfloat16)
            if d == 0:
                h1r[r, f, here] = rows
            else:
                h1s[r, f, d - 1] = rows
                h1_copy(r, f, d).start()

    def h2_begin(r, f):
        arrived(h1s.at[r, f], h1recv.at[r, f])
        block = h1r[r, f].reshape(N * PAIR, CW)
        for d in (2, 1, 3, 0):
            to = (y + d) % N if r else d
            pick = m2[r, pl.ds(pl.multiple_of(to * ROWS, ROWS), ROWS), :]
            h2s[r, f, d] = jnp.dot(pick, block, preferred_element_type=jnp.float32).astype(jnp.bfloat16)
            if r and d:
                h2_copy(f, d).start()
        if r == 0:

            @pl.when(z == 0)
            def _():
                for to in (3, 2, 1):
                    z_copy(f, to, 0).start()

            @pl.when(z == 3)
            def _():
                for to in (0, 1, 2):
                    z_copy(f, to, 1).start()

    def add_on(f, to, way):
        slot = (z - to) if way else (to - z)
        z_arrival(f, slot, way).wait_recv()
        h2s[0, f, to] = h2s[0, f, to] + zpart[f, way, slot]
        z_copy(f, to, way).start()

    def merge_first(f):
        @pl.when(z == 1)
        def _():
            add_on(f, 3, 0)
            add_on(f, 2, 0)

        @pl.when(z == 2)
        def _():
            add_on(f, 0, 1)
            add_on(f, 1, 1)

    def merge_second(f):
        @pl.when(z == 2)
        def _():
            add_on(f, 3, 0)

        @pl.when(z == 1)
        def _():
            add_on(f, 0, 1)

    def hand_out(r, f):
        @pl.when(core == 1 - r)
        def _():
            emit(r, f, ahead_out).start()

        @pl.when(core == r)
        def _():
            emit(r, f, behind_out).start()

    def finish_local(f):
        result[0, f] = h2s[0, f, z]

        @pl.when(z > 0)
        def _():
            z_arrival(f, 0, 0).wait_recv()
            result[0, f] = result[0, f] + zpart[f, 0, 0]

        @pl.when(z < 3)
        def _():
            z_arrival(f, 0, 1).wait_recv()
            result[0, f] = result[0, f] + zpart[f, 1, 0]

        hand_out(0, f)

    def finish_cross(f):
        arrived(last.at[f], h2recv.at[f])
        result[1, f] = (h2s[1, f, 0] + last[f, 0]) + (last[f, 1] + last[f, 2])
        hand_out(1, f)

    G1, G2, G3 = 128, 32, 16

    def axis_of(n, h):
        return "xy"[(n + h) % 2]

    def at(axis):
        return x if axis == "x" else y

    def g1_copy(h, d):
        axis = axis_of(0, h)
        to = (at(axis) + d) % N
        return remote(
            grads.at[pl.ds(h * 512 + to * G1, G1)], g1.at[h, d - 1], gsend.at[0, h, d - 1], grecv.at[0, h, d - 1],
            along[axis][d],
        )

    def g2_copy(h, d):
        axis = axis_of(1, h)
        to = (at(axis) + d) % N
        return remote(
            g1_sum.at[h, pl.ds(to * G2, G2)], g2.at[h, d - 1], gsend.at[1, h, d - 1], grecv.at[1, h, d - 1],
            along[axis][d],
        )

    def g3_copy(d):
        to = (z + d) % N
        return remote(
            total.at[pl.ds(to * G3, G3)], g3.at[d - 1], gsend.at[2, 0, d - 1], grecv.at[2, 0, d - 1], me.in_block(dz=d)
        )

    def add_three(own, parts):
        return (own + parts[0].astype(jnp.float32)) + (parts[1].astype(jnp.float32) + parts[2].astype(jnp.float32))

    def grads_first():
        for h in (0, 1):
            for d in others:
                g1_copy(h, d).start()

    def grads_second():
        for h in (0, 1):
            for d in others:
                g1_copy(h, d).wait_recv()
            row = pl.multiple_of(h * 512 + at(axis_of(0, h)) * G1, G1)
            g1_sum[h] = add_three(grads[pl.ds(row, G1), :].astype(jnp.float32), g1[h])
            for d in others:
                g2_copy(h, d).start()

    def grads_third():
        for h in (0, 1):
            for d in others:
                g2_copy(h, d).wait_recv()
            row = pl.multiple_of(at(axis_of(1, h)) * G2, G2)
            total[pl.ds(h * G2, G2), :] = add_three(g1_sum[h, pl.ds(row, G2), :], g2[h])
        for d in others:
            g3_copy(d).start()

    def grads_last():
        for d in others:
            g3_copy(d).wait_recv()
        both = add_three(total[pl.ds(pl.multiple_of(z * G3, G3), G3), :], g3[...])
        for j in range(8):
            down_out[:, j * LANE : (j + 1) * LANE] = both[j : j + 1]
            up_out[:, j * LANE : (j + 1) * LANE] = both[8 + j : 9 + j]

    steps = {
        "cross_start": lambda f: cross_copy(f).start(),
        "local_start": local_start,
        "local_pick": lambda f: h1_begin(0, f),
        "merge_first": merge_first,
        "merge_second": merge_second,
        "cross_pass": pass_on,
        "cross_pick": lambda f: h1_begin(1, f),
        "local_sort": lambda f: h2_begin(0, f),
        "cross_sort": lambda f: h2_begin(1, f),
        "cross_end": finish_cross,
        "local_end": finish_local,
    }
    for name, lag in PLAN:
        for f in range(min(-lag, NC)):
            steps[name](f)
    for r, (receivers, spots) in enumerate(((local1, local2), (cross1, cross2))):
        i = lax.broadcasted_iota(jnp.int32, (N * N * N, N * SLOTS), 0)
        c = lax.broadcasted_iota(jnp.int32, (N * N * N, N * SLOTS), 1) // SLOTS
        if r:
            to, fits = (i // N) * N + z, i % N == jnp.where(core == 1, 3 - c, c)
        else:
            to, fits = x * 16 + (i // 16) * N + i % N, (i // N) % N == c
        hit = fits & (receivers[...] == (to + 1).astype(jnp.float32))
        m1[r] = spread_tokens(jnp.where(hit, 1.0, 0.0).astype(jnp.bfloat16))
        i = lax.broadcasted_iota(jnp.int32, (N * SLOTS, N * N * N), 0)
        c = lax.broadcasted_iota(jnp.int32, (N * SLOTS, N * N * N), 1)
        spot = jnp.dot(
            repeat_matrix(N * SLOTS, N, SLOTS, 0), spots[...].astype(jnp.bfloat16), preferred_element_type=jnp.float32
        )
        fits = i // SLOTS == ((c // N) % N if r else c % N)
        hit = fits & (spot == (i % SLOTS).astype(jnp.float32))
        m2[r] = spread_tokens(jnp.where(hit, 1.0, 0.0).astype(jnp.bfloat16))

    def turn(n, _):
        for name, lag in PLAN:
            if name == "grads":
                for when, run in zip(GRADS, (grads_first, grads_second, grads_third)):
                    pl.when(n == when)(run)
            elif -lag < NC:
                pl.when((n >= lag) & (n < NC + lag))(functools.partial(steps[name], n - lag))
        return 0

    lax.fori_loop(0, NC + max(lag for _, lag in PLAN), turn, 0)
    grads_last()

    for d in others:
        for h in (0, 1):
            g1_copy(h, d).wait_send()
            g2_copy(h, d).wait_send()
        g3_copy(d).wait_send()

    left(lbuf, 0)
    left(src.at[0], 1)
    pl.when(o < 3)(lambda: left(dbuf, 2))
    left(h1s, 3)
    left(last, 4)
    left(last, 5)
    pltpu.make_async_copy(result, result, out_sem).wait()


def route(routed, local1, local2, cross1, cross2, grads):
    bf16, f32 = jnp.bfloat16, jnp.float32
    vmem, dma = pltpu.VMEM, pltpu.SemaphoreType.DMA
    scratch = [
        vmem((NC, N, ROWS, CW), bf16),
        vmem((NC, N, ROWS, CW), bf16),
        vmem((2, NC, 3, PAIR, CW), bf16),
        vmem((2, NC, N, PAIR, CW), bf16),
        vmem((2, NC, N, ROWS, CW), bf16),
        vmem((NC, 3, ROWS, CW), bf16),
        vmem((NC, 2, 3, ROWS, CW), bf16),
        vmem((2, NC, ROWS, CW), bf16),
        vmem((2, N * PAIR, N * ROWS), bf16),
        vmem((2, N * ROWS, N * PAIR), bf16),
        vmem((2, 3, 128, LANE), bf16),
        vmem((2, 128, LANE), f32),
        vmem((2, 3, 32, LANE), f32),
        vmem((3, 16, LANE), f32),
        vmem((64, LANE), f32),
        dma((6,)),
        dma((NC,)), dma((NC, N)),
        dma((2, NC)), dma((NC,)), dma((NC, 2, 3)),
        dma,
        dma((3, 2, 3)), dma((3, 2, 3)),
    ]
    return pl.pallas_call(
        route_kernel,
        out_shape=(
            jax.ShapeDtypeStruct((ROWS, D), bf16),
            jax.ShapeDtypeStruct((ROWS, D), bf16),
            jax.ShapeDtypeStruct((1, D), f32),
            jax.ShapeDtypeStruct((1, D), f32),
        ),
        in_specs=[pl.BlockSpec(memory_space=pltpu.VMEM)] * 6,
        out_specs=(
            pl.BlockSpec(memory_space=pl.ANY),
            pl.BlockSpec(memory_space=pl.ANY),
            pl.BlockSpec(memory_space=pltpu.VMEM),
            pl.BlockSpec(memory_space=pltpu.VMEM),
        ),
        scratch_shapes=scratch,
        compiler_params=pltpu.CompilerParams(
            collective_id=1, has_side_effects=True, vmem_limit_bytes=48 * MIB
        ),
        name="route",
    )(routed, local1, local2, cross1, cross2, grads)


def pool_order(halves):
    rest = halves.shape[2:]
    first = halves[0].reshape((N, N, 2) + rest)
    second = jnp.swapaxes(halves[1].reshape((N, N, 2) + rest), 0, 1)
    return jnp.concatenate([first, second], axis=2).reshape((R,) + rest)


def picks(tables, crossing):
    me = Place()
    grid = tables.reshape(N, N, N, SLOTS)
    coord = jnp.arange(N, dtype=jnp.int32)
    if crossing:
        group, mine = grid[me.x, me.y], me.x * 16 + coord * 4 + me.z + 1
        group = jnp.where(me.core == 1, group[::-1], group)
    else:
        group, mine = grid[:, me.y, me.z], me.x * 16 + me.y * 4 + coord + 1
    sent = jnp.any(tables[None] == mine[:, None, None], axis=2)
    spot = jnp.cumsum(sent.astype(jnp.int32), axis=1) - 1
    spot = jnp.where(sent, spot, -1).astype(jnp.float32).reshape(N, N, N, N)
    if crossing:
        spot = lax.dynamic_index_in_dim(spot, me.y, 2, keepdims=True)
    else:
        spot = lax.dynamic_index_in_dim(spot, me.z, 3, keepdims=True)
        spot = jnp.swapaxes(spot, 1, 2)
    spot = jnp.broadcast_to(spot, (N, N, N, N)).reshape(N, N * N * N)
    return group.astype(jnp.float32).reshape(1, N * SLOTS), spot


def shards(
    activations, cotangents, token_counts, route_ahead, route_back, down_rows, up_rows, norm_gain
):
    sizes = token_counts[0, 0, :SLOTS]
    live = sizes > 0
    entry = [jnp.where(live, to[0, 0, :SLOTS] + 1, 0).astype(jnp.bfloat16) for to in (route_ahead, route_back)]
    table = jnp.concatenate(
        [jnp.pad(row[None], ((i, 15 - i), (0, 128 - SLOTS))) for i, row in enumerate(entry)], axis=0
    )
    own = jnp.stack([down_rows[0, 0], up_rows[0, 0]]).reshape(16, LANE)
    full, tables = gather(own, table)
    full = full.reshape(R, 16, LANE)
    down_full, up_full = full[:, :8].reshape(R, D), full[:, 8:].reshape(R, D)
    section = lax.axis_index("section")
    tables = pool_order(tables[:, :, :2, :SLOTS].astype(jnp.int32))
    from_prev = jnp.where(section > 0, tables[:, 0], 0)
    from_next = jnp.where(section < lax.axis_size("section") - 1, tables[:, 1], 0)

    rows = activations.reshape(-1, D)
    grads = cotangents.reshape(-1, D)
    keep = (jnp.arange(TOK, dtype=jnp.int32)[None, :] < sizes[:, None]).astype(jnp.float32).reshape(ROWS, 1)
    routed, grad_down, grad_up = adapter(rows, grads, keep, down_full, up_full, norm_gain)

    odd = section % 2 == 1
    local, cross = jnp.where(odd, from_prev, from_next), jnp.where(odd, from_next, from_prev)
    local1, local2 = picks(local, False)
    cross1, cross2 = picks(cross, True)
    share = jnp.concatenate([grad_down.reshape(R, 8, LANE), grad_up.reshape(R, 8, LANE)], axis=1)
    ahead, behind, sum_down, sum_up = route(routed, local1, local2, cross1, cross2, share.reshape(R * 16, LANE))
    shape = (1, 1, SLOTS, TOK, D)
    return (ahead.reshape(shape), behind.reshape(shape), sum_down[None], sum_up[None])


def solution(mesh):
    placed = (
        P("section", "pool", None, None, None),
        P("section", "pool", None, None, None),
        P("section", "pool", None),
        P("section", "pool", None),
        P("section", "pool", None),
        P("section", "pool", None),
        P("section", "pool", None),
        P("section", None),
    )
    return jax.shard_map(
        shards,
        mesh=mesh,
        in_specs=placed,
        out_specs=(
            P("section", "pool", None, None, None),
            P("section", "pool", None, None, None),
            P("section", "pool", None),
            P("section", "pool", None),
        ),
        check_vma=False,
    )
```

```python
import functools

import jax
import jax.numpy as jnp
from jax import lax
from jax.experimental import pallas as pl
from jax.experimental.pallas import tpu as pltpu
from jax.sharding import PartitionSpec as P

SLOTS = 12
TOK = 8
ROWS = SLOTS * TOK
N = 4
D = 5120
R = 64
NC = 10
CW = D // NC
LANE = 640
epsilon = 1e-05
MIB = 1 << 20


class Place:
    def __init__(self):
        section = lax.axis_index("section")
        pool = lax.axis_index("pool")
        self.section, self.pool = section, pool
        self.block, self.core = section // 2, section % 2
        self.x, self.y, self.z = pool // 16, (pool // 4) % 4, pool % 4

    def in_block(self, dx=0, dy=0, dz=0):
        x, y, z = (self.x + dx) % N, (self.y + dy) % N, (self.z + dz) % N
        return {"section": self.section, "pool": x * 16 + y * 4 + z}

    def along_z(self, step):
        far = (self.block * N + self.z + step + 4 * N) % (4 * N)
        return {"section": (far // N) * 2 + self.core, "pool": self.pool - self.z + far % N}


def greet(peers):
    barrier = pltpu.get_barrier_semaphore()
    for peer in peers:
        pl.semaphore_signal(barrier, inc=1, device_id=peer, device_id_type=pl.DeviceIdType.MESH)
    pl.semaphore_wait(barrier, len(peers))


def remote(src, dst, send, recv, peer):
    return pltpu.make_async_remote_copy(
        src_ref=src, dst_ref=dst, send_sem=send, recv_sem=recv, device_id=peer, device_id_type=pl.DeviceIdType.MESH
    )


def gather_kernel(own_ref, table_ref, full_ref, tables_ref, tin, both, tin_send, tin_recv, send_sems, recv_sems):
    me = Place()
    x, y, z = me.x, me.y, me.z
    others = (1, 2, 3)
    to_next = {"section": (me.section + 1) % 8, "pool": me.pool}
    to_prev = {"section": (me.section + 7) % 8, "pool": me.pool}
    along = {
        "x": {d: me.in_block(dx=d) for d in others},
        "y": {d: me.in_block(dy=d) for d in others},
        "z": {d: me.in_block(dz=d) for d in others},
    }
    greet([to_next, to_prev] + [along[axis][d] for axis in "xyz" for d in others])

    crossing = [
        remote(table_ref.at[pl.ds(0, 16)], tin.at[pl.ds(0, 16)], tin_send.at[0], tin_recv.at[0], to_next),
        remote(table_ref.at[pl.ds(16, 16)], tin.at[pl.ds(16, 16)], tin_send.at[1], tin_recv.at[1], to_prev),
    ]
    for copy in crossing:
        copy.start()

    half, k = z // 2, z % 2
    place = jnp.where(half == 0, x * 8 + y * 2, y * 8 + x * 2)

    def spread(a, own, full):
        for d in others:
            remote(own, full.at[half, place + k], send_sems.at[a, 0], recv_sems.at[a, 0], along["z"][d]).start()
        full[half, place + k] = own[...]

    def group(a, full, n, size, h, wait):
        view = full.at[h, pl.ds(0, 3 * size)]
        sem = 0 if n < 0 else 1 + 2 * n + h
        copy = remote(view, view, send_sems.at[a, sem], recv_sems.at[a, sem], along["z"][1])
        copy.wait_recv() if wait else copy.wait_send()

    def collect(a, own, full):
        group(a, full, -1, 1, 0, True)

    def stage(a, full, n, wait):
        size = (2, 8)[n]
        for h in (0, 1):
            first, second = ((y, x), (x, y))[h]
            axis = ("yx", "xy")[h][n]
            at = (second * 8 + first * 2) if n == 0 else second * 8
            if wait:
                group(a, full, n, size, h, True)
                continue
            for d in (2, 1, 3):
                view = full.at[h, pl.ds(at, size)]
                sem = 1 + 2 * n + h
                remote(view, view, send_sems.at[a, sem], recv_sems.at[a, sem], along[axis][d]).start()

    weights = (0, own_ref, full_ref)
    marks = (1, both, tables_ref)
    spread(*weights)
    for copy in crossing:
        copy.wait_recv()
    both[...] = tin[:16] + tin[16:]
    spread(*marks)
    collect(*weights)
    stage(0, full_ref, 0, False)
    collect(*marks)
    stage(1, tables_ref, 0, False)
    stage(0, full_ref, 0, True)
    stage(0, full_ref, 1, False)
    stage(1, tables_ref, 0, True)
    stage(1, tables_ref, 1, False)
    stage(0, full_ref, 1, True)
    stage(1, tables_ref, 1, True)
    for copy in crossing:
        copy.wait_send()
    for a, full in ((0, full_ref), (1, tables_ref)):
        group(a, full, -1, 1, 0, False)
        for n, size in ((0, 2), (1, 8)):
            for h in (0, 1):
                group(a, full, n, size, h, False)


def gather(own, table):
    dma = pltpu.SemaphoreType.DMA
    return pl.pallas_call(
        gather_kernel,
        out_shape=(
            jax.ShapeDtypeStruct((2, R // 2, 16, LANE), jnp.bfloat16),
            jax.ShapeDtypeStruct((2, R // 2, 16, 128), jnp.bfloat16),
        ),
        in_specs=[pl.BlockSpec(memory_space=pltpu.VMEM)] * 2,
        out_specs=(pl.BlockSpec(memory_space=pltpu.VMEM),) * 2,
        scratch_shapes=[
            pltpu.VMEM((32, 128), jnp.bfloat16), pltpu.VMEM((16, 128), jnp.bfloat16),
            dma((2,)), dma((2,)), dma((2, 5)), dma((2, 5)),
        ],
        compiler_params=pltpu.CompilerParams(
            collective_id=0, has_side_effects=True, vmem_limit_bytes=16 * MIB
        ),
        name="gather",
    )(own, table)


def adapter_kernel(x_ref, g_ref, keep_ref, down_ref, up_ref, gain_ref, routed_ref, gd_ref, gu_ref, normed, through):
    keep = keep_ref[...] > 0.0
    square = jnp.zeros((ROWS, 1), jnp.float32)
    for f in range(NC):
        wide = x_ref[:, f * CW : (f + 1) * CW].astype(jnp.float32)
        square += jnp.sum(wide * wide, axis=1, keepdims=True)
    inv_rms = lax.rsqrt(square * (1.0 / D) + epsilon)
    across = (((1,), (1,)), ((), ()))
    preact = jnp.zeros((ROWS, R), jnp.float32)
    back = jnp.zeros((ROWS, R), jnp.float32)
    for f in range(NC):
        cols = slice(f * CW, (f + 1) * CW)
        wide = x_ref[:, cols].astype(jnp.float32)
        part = (wide * inv_rms * gain_ref[:, cols].astype(jnp.float32)).astype(jnp.bfloat16)
        normed[:, cols] = part
        preact += lax.dot_general(part, down_ref[:, cols], across, preferred_element_type=jnp.float32)
        grad = jnp.where(keep, g_ref[:, cols].astype(jnp.float32), 0.0).astype(jnp.bfloat16)
        back += lax.dot_general(grad, up_ref[:, cols], across, preferred_element_type=jnp.float32)
    gates = jax.nn.sigmoid(preact)
    hidden_wide = (preact * gates).astype(jnp.bfloat16).astype(jnp.float32)
    slope_wide = (back * gates * (1.0 + preact * (1.0 - gates))).astype(jnp.bfloat16).astype(jnp.float32)
    hidden, slope = hidden_wide.astype(jnp.bfloat16), slope_wide.astype(jnp.bfloat16)
    hidden_t, slope_t = hidden_wide.T.astype(jnp.bfloat16), slope_wide.T.astype(jnp.bfloat16)
    centred = jnp.zeros((ROWS, 1), jnp.float32)
    for f in range(NC):
        cols = slice(f * CW, (f + 1) * CW)
        wide = x_ref[:, cols].astype(jnp.float32)
        branch = jnp.dot(hidden, up_ref[:, cols], preferred_element_type=jnp.float32)
        routed_ref[0, f] = jnp.where(keep, wide + branch, 0.0).astype(jnp.bfloat16)
        grad = jnp.where(keep, g_ref[:, cols].astype(jnp.float32), 0.0).astype(jnp.bfloat16)
        gu_ref[:, cols] = jnp.dot(hidden_t, grad, preferred_element_type=jnp.float32).astype(jnp.bfloat16)
        gd_ref[:, cols] = jnp.dot(slope_t, normed[:, cols], preferred_element_type=jnp.float32).astype(jnp.bfloat16)
        part = jnp.dot(slope, down_ref[:, cols], preferred_element_type=jnp.float32)
        part = part * gain_ref[:, cols].astype(jnp.float32)
        through[:, cols] = part
        centred += jnp.sum(part * wide, axis=1, keepdims=True)
    centred = centred * (1.0 / D)
    for f in range(NC):
        cols = slice(f * CW, (f + 1) * CW)
        wide = x_ref[:, cols].astype(jnp.float32)
        grad = jnp.where(keep, g_ref[:, cols].astype(jnp.float32), 0.0)
        inward = grad + inv_rms * (through[:, cols] - wide * inv_rms * inv_rms * centred)
        routed_ref[1, f] = inward.astype(jnp.bfloat16)


def adapter(rows, grads, keep, down_full, up_full, gain_row):
    whole = lambda shape: pl.BlockSpec(shape, lambda i: (0,) * len(shape))
    return pl.pallas_call(
        adapter_kernel,
        grid=(1,),
        out_shape=(
            jax.ShapeDtypeStruct((2, NC, ROWS, CW), jnp.bfloat16),
            jax.ShapeDtypeStruct((R, D), jnp.bfloat16),
            jax.ShapeDtypeStruct((R, D), jnp.bfloat16),
        ),
        in_specs=[
            whole((ROWS, D)),
            whole((ROWS, D)),
            whole((ROWS, 1)),
            whole((R, D)),
            whole((R, D)),
            whole((1, D)),
        ],
        out_specs=(whole((2, NC, ROWS, CW)), whole((R, D)), whole((R, D))),
        scratch_shapes=[pltpu.VMEM((ROWS, D), jnp.bfloat16), pltpu.VMEM((ROWS, D), jnp.float32)],
        compiler_params=pltpu.CompilerParams(vmem_limit_bytes=40 * MIB),
        cost_estimate=pl.CostEstimate(flops=6 * 2 * ROWS * R * D, bytes_accessed=10 * MIB, transcendentals=ROWS * R),
        name="adapter",
    )(rows, grads, keep, down_full, up_full, gain_row)


def repeat_matrix(rows, cols, times, along):
    r = lax.broadcasted_iota(jnp.int32, (rows, cols), 0)
    c = lax.broadcasted_iota(jnp.int32, (rows, cols), 1)
    return ((r // times == c) if along == 0 else (c // times == r)).astype(jnp.bfloat16)


def spread_tokens(small):
    a, b = small.shape
    tall = jnp.dot(repeat_matrix(TOK * a, a, TOK, 0), small, preferred_element_type=jnp.float32).astype(jnp.bfloat16)
    wide = jnp.dot(tall, repeat_matrix(b, TOK * b, TOK, 1), preferred_element_type=jnp.float32)
    r = lax.broadcasted_iota(jnp.int32, (TOK * a, TOK * b), 0) % TOK
    c = lax.broadcasted_iota(jnp.int32, (TOK * a, TOK * b), 1) % TOK
    return jnp.where(r == c, wide, 0.0).astype(jnp.bfloat16)


PAIR = N * N * TOK
PLAN = (
    ("cross_start", -2),
    ("local_start", -3),
    ("cross_pass", 0),
    ("merge_first", 4),
    ("merge_second", 6),
    ("local_pick", 0),
    ("cross_pick", 1),
    ("local_sort", 2),
    ("grads", 0),
    ("cross_sort", 3),
    ("cross_end", 5),
    ("local_end", 8),
)
GRADS = (2, 4, 6)


def route_kernel(
    src, local1, local2, cross1, cross2, grads,
    ahead_out, behind_out, down_out, up_out,
    lbuf, dbuf, h1s, h1r, h2s, last, zpart, result, m1, m2,
    g1, g1_sum, g2, g3, total,
    sent, lrecv, drecv, h1recv, h2recv, zrecv, out_sem,
    gsend, grecv,
):
    me = Place()
    x, y, z, core = me.x, me.y, me.z, me.core
    o = jnp.where(core == 0, z, 3 - z)
    znext = me.along_z(1 - 2 * core)
    others = (1, 2, 3)
    along = {"x": {d: me.in_block(dx=d) for d in others}, "y": {d: me.in_block(dy=d) for d in others}}
    zup, zdown = me.in_block(dz=1), me.in_block(dz=3)
    other_core = me.section + 1 - 2 * core

    def facing(d):
        return {"section": other_core, "pool": ((x + d) % N) * 16 + y * 4 + z}

    entry = {
        "section": ((me.block + 2 * core - 1 + N) % N) * 2 + 1 - core,
        "pool": me.pool - z + 3 * (1 - core),
    }
    so = jnp.where(core == 1, z, 3 - z)

    barrier = pltpu.get_barrier_semaphore()

    def hello(peer):
        pl.semaphore_signal(barrier, inc=1, device_id=peer, device_id_type=pl.DeviceIdType.MESH)

    everyone = [me.in_block(dz=d) for d in others] + [along["x"][d] for d in others] + [along["y"][d] for d in others]
    everyone += [znext, me.along_z(2 * core - 1)]
    everyone += [facing(d) for d in range(N)]
    for way in (1, N - 1):
        for k in range(N):
            everyone.append({"section": ((me.block + way) % N) * 2 + 1 - core, "pool": me.pool - z + k})
    for peer in everyone:
        hello(peer)
    pl.semaphore_wait(barrier, len(everyone))

    def local_copy(f, d):
        return remote(src.at[core, f], lbuf.at[f, x], sent.at[0], lrecv.at[f], facing(d))

    def cross_copy(f):
        return remote(src.at[1 - core, f], dbuf.at[f, so], sent.at[1], drecv.at[f, so], entry)

    def cross_pass(f, k):
        return remote(dbuf.at[f, k], dbuf.at[f, k], sent.at[2], drecv.at[f, k], znext)

    def h1_copy(r, f, d):
        return remote(
            h1s.at[r, f, d - 1], h1r.at[r, f, x if r else y], sent.at[3], h1recv.at[r, f],
            along["x" if r else "y"][d],
        )

    def h2_copy(f, d):
        return remote(h2s.at[1, f, d], last.at[f, d - 1], sent.at[4], h2recv.at[f], along["y"][d])

    def z_copy(f, to, way):
        slot = (z - to - 1) if way else (to - z - 1)
        return remote(
            h2s.at[0, f, to], zpart.at[f, way, slot], sent.at[5], zrecv.at[f, way, slot], zdown if way else zup
        )

    def z_arrival(f, slot, way):
        return remote(
            h2s.at[0, f, 0], zpart.at[f, way, slot], sent.at[5], zrecv.at[f, way, slot], zdown if way else zup
        )

    def arrived(ref, sem):
        remote(ref, ref, sent.at[0], sem, zup).wait_recv()

    def left(ref, n):
        remote(ref, ref, sent.at[n], zrecv.at[0, 0, 0], zup).wait_send()

    def emit(r, f, out):
        cols = pl.ds(pl.multiple_of(f * CW, 128), CW)
        return pltpu.make_async_copy(result.at[r, f], out.at[:, cols], out_sem)

    def local_start(f):
        for d in (2, 1, 3, 0):
            local_copy(f, d).start()

    def pass_on(f):
        for k in (3, 2, 1, 0):
            cross_pass(f, k).wait_recv()

            @pl.when(o < 3)
            def _():
                cross_pass(f, k).start()

    def h1_begin(r, f):
        if r == 0:
            arrived(lbuf.at[f], lrecv.at[f])
        here = x if r else y
        block = (dbuf if r else lbuf)[f].reshape(N * ROWS, CW)
        for d in (2, 1, 3, 0):
            to = (here + d) % N
            pick = m1[r, pl.ds(pl.multiple_of(to * PAIR, PAIR), PAIR), :]
            rows = jnp.dot(pick, block, preferred_element_type=jnp.float32).astype(jnp.bfloat16)
            if d == 0:
                h1r[r, f, here] = rows
            else:
                h1s[r, f, d - 1] = rows
                h1_copy(r, f, d).start()

    def h2_begin(r, f):
        arrived(h1s.at[r, f], h1recv.at[r, f])
        block = h1r[r, f].reshape(N * PAIR, CW)
        for d in (2, 1, 3, 0):
            to = (y + d) % N if r else d
            pick = m2[r, pl.ds(pl.multiple_of(to * ROWS, ROWS), ROWS), :]
            h2s[r, f, d] = jnp.dot(pick, block, preferred_element_type=jnp.float32).astype(jnp.bfloat16)
            if r and d:
                h2_copy(f, d).start()
        if r == 0:

            @pl.when(z == 0)
            def _():
                for to in (3, 2, 1):
                    z_copy(f, to, 0).start()

            @pl.when(z == 3)
            def _():
                for to in (0, 1, 2):
                    z_copy(f, to, 1).start()

    def add_on(f, to, way):
        slot = (z - to) if way else (to - z)
        z_arrival(f, slot, way).wait_recv()
        h2s[0, f, to] = h2s[0, f, to] + zpart[f, way, slot]
        z_copy(f, to, way).start()

    def merge_first(f):
        @pl.when(z == 1)
        def _():
            add_on(f, 3, 0)
            add_on(f, 2, 0)

        @pl.when(z == 2)
        def _():
            add_on(f, 0, 1)
            add_on(f, 1, 1)

    def merge_second(f):
        @pl.when(z == 2)
        def _():
            add_on(f, 3, 0)

        @pl.when(z == 1)
        def _():
            add_on(f, 0, 1)

    def hand_out(r, f):
        @pl.when(core == 1 - r)
        def _():
            emit(r, f, ahead_out).start()

        @pl.when(core == r)
        def _():
            emit(r, f, behind_out).start()

    def finish_local(f):
        result[0, f] = h2s[0, f, z]

        @pl.when(z > 0)
        def _():
            z_arrival(f, 0, 0).wait_recv()
            result[0, f] = result[0, f] + zpart[f, 0, 0]

        @pl.when(z < 3)
        def _():
            z_arrival(f, 0, 1).wait_recv()
            result[0, f] = result[0, f] + zpart[f, 1, 0]

        hand_out(0, f)

    def finish_cross(f):
        arrived(last.at[f], h2recv.at[f])
        result[1, f] = (h2s[1, f, 0] + last[f, 0]) + (last[f, 1] + last[f, 2])
        hand_out(1, f)

    G1, G2, G3 = 128, 32, 16

    def axis_of(n, h):
        return "xy"[(n + h) % 2]

    def at(axis):
        return x if axis == "x" else y

    def g1_copy(h, d):
        axis = axis_of(0, h)
        to = (at(axis) + d) % N
        return remote(
            grads.at[pl.ds(h * 512 + to * G1, G1)], g1.at[h, d - 1], gsend.at[0, h, d - 1], grecv.at[0, h, d - 1],
            along[axis][d],
        )

    def g2_copy(h, d):
        axis = axis_of(1, h)
        to = (at(axis) + d) % N
        return remote(
            g1_sum.at[h, pl.ds(to * G2, G2)], g2.at[h, d - 1], gsend.at[1, h, d - 1], grecv.at[1, h, d - 1],
            along[axis][d],
        )

    def g3_copy(d):
        to = (z + d) % N
        return remote(
            total.at[pl.ds(to * G3, G3)], g3.at[d - 1], gsend.at[2, 0, d - 1], grecv.at[2, 0, d - 1], me.in_block(dz=d)
        )

    def add_three(own, parts):
        return (own + parts[0].astype(jnp.float32)) + (parts[1].astype(jnp.float32) + parts[2].astype(jnp.float32))

    def grads_first():
        for h in (0, 1):
            for d in others:
                g1_copy(h, d).start()

    def grads_second():
        for h in (0, 1):
            for d in others:
                g1_copy(h, d).wait_recv()
            row = pl.multiple_of(h * 512 + at(axis_of(0, h)) * G1, G1)
            g1_sum[h] = add_three(grads[pl.ds(row, G1), :].astype(jnp.float32), g1[h])
            for d in others:
                g2_copy(h, d).start()

    def grads_third():
        for h in (0, 1):
            for d in others:
                g2_copy(h, d).wait_recv()
            row = pl.multiple_of(at(axis_of(1, h)) * G2, G2)
            total[pl.ds(h * G2, G2), :] = add_three(g1_sum[h, pl.ds(row, G2), :], g2[h])
        for d in others:
            g3_copy(d).start()

    def grads_last():
        for d in others:
            g3_copy(d).wait_recv()
        both = add_three(total[pl.ds(pl.multiple_of(z * G3, G3), G3), :], g3[...])
        for j in range(8):
            down_out[:, j * LANE : (j + 1) * LANE] = both[j : j + 1]
            up_out[:, j * LANE : (j + 1) * LANE] = both[8 + j : 9 + j]

    steps = {
        "cross_start": lambda f: cross_copy(f).start(),
        "local_start": local_start,
        "local_pick": lambda f: h1_begin(0, f),
        "merge_first": merge_first,
        "merge_second": merge_second,
        "cross_pass": pass_on,
        "cross_pick": lambda f: h1_begin(1, f),
        "local_sort": lambda f: h2_begin(0, f),
        "cross_sort": lambda f: h2_begin(1, f),
        "cross_end": finish_cross,
        "local_end": finish_local,
    }
    for name, lag in PLAN:
        for f in range(min(-lag, NC)):
            steps[name](f)
    for r, (receivers, spots) in enumerate(((local1, local2), (cross1, cross2))):
        i = lax.broadcasted_iota(jnp.int32, (N * N * N, N * SLOTS), 0)
        c = lax.broadcasted_iota(jnp.int32, (N * N * N, N * SLOTS), 1) // SLOTS
        if r:
            to, fits = (i // N) * N + z, i % N == jnp.where(core == 1, 3 - c, c)
        else:
            to, fits = x * 16 + (i // 16) * N + i % N, (i // N) % N == c
        hit = fits & (receivers[...] == (to + 1).astype(jnp.float32))
        m1[r] = spread_tokens(jnp.where(hit, 1.0, 0.0).astype(jnp.bfloat16))
        i = lax.broadcasted_iota(jnp.int32, (N * SLOTS, N * N * N), 0)
        c = lax.broadcasted_iota(jnp.int32, (N * SLOTS, N * N * N), 1)
        spot = jnp.dot(
            repeat_matrix(N * SLOTS, N, SLOTS, 0), spots[...].astype(jnp.bfloat16), preferred_element_type=jnp.float32
        )
        fits = i // SLOTS == ((c // N) % N if r else c % N)
        hit = fits & (spot == (i % SLOTS).astype(jnp.float32))
        m2[r] = spread_tokens(jnp.where(hit, 1.0, 0.0).astype(jnp.bfloat16))

    def turn(n, _):
        for name, lag in PLAN:
            if name == "grads":
                for when, run in zip(GRADS, (grads_first, grads_second, grads_third)):
                    pl.when(n == when)(run)
            elif -lag < NC:
                pl.when((n >= lag) & (n < NC + lag))(functools.partial(steps[name], n - lag))
        return 0

    lax.fori_loop(0, NC + max(lag for _, lag in PLAN), turn, 0)
    grads_last()

    for d in others:
        for h in (0, 1):
            g1_copy(h, d).wait_send()
            g2_copy(h, d).wait_send()
        g3_copy(d).wait_send()

    left(lbuf, 0)
    left(src.at[0], 1)
    pl.when(o < 3)(lambda: left(dbuf, 2))
    left(h1s, 3)
    left(last, 4)
    left(last, 5)
    pltpu.make_async_copy(result, result, out_sem).wait()


def route(routed, local1, local2, cross1, cross2, grads):
    bf16, f32 = jnp.bfloat16, jnp.float32
    vmem, dma = pltpu.VMEM, pltpu.SemaphoreType.DMA
    scratch = [
        vmem((NC, N, ROWS, CW), bf16),
        vmem((NC, N, ROWS, CW), bf16),
        vmem((2, NC, 3, PAIR, CW), bf16),
        vmem((2, NC, N, PAIR, CW), bf16),
        vmem((2, NC, N, ROWS, CW), bf16),
        vmem((NC, 3, ROWS, CW), bf16),
        vmem((NC, 2, 3, ROWS, CW), bf16),
        vmem((2, NC, ROWS, CW), bf16),
        vmem((2, N * PAIR, N * ROWS), bf16),
        vmem((2, N * ROWS, N * PAIR), bf16),
        vmem((2, 3, 128, LANE), bf16),
        vmem((2, 128, LANE), f32),
        vmem((2, 3, 32, LANE), f32),
        vmem((3, 16, LANE), f32),
        vmem((64, LANE), f32),
        dma((6,)),
        dma((NC,)), dma((NC, N)),
        dma((2, NC)), dma((NC,)), dma((NC, 2, 3)),
        dma,
        dma((3, 2, 3)), dma((3, 2, 3)),
    ]
    return pl.pallas_call(
        route_kernel,
        out_shape=(
            jax.ShapeDtypeStruct((ROWS, D), bf16),
            jax.ShapeDtypeStruct((ROWS, D), bf16),
            jax.ShapeDtypeStruct((1, D), f32),
            jax.ShapeDtypeStruct((1, D), f32),
        ),
        in_specs=[pl.BlockSpec(memory_space=pltpu.VMEM)] * 6,
        out_specs=(
            pl.BlockSpec(memory_space=pl.ANY),
            pl.BlockSpec(memory_space=pl.ANY),
            pl.BlockSpec(memory_space=pltpu.VMEM),
            pl.BlockSpec(memory_space=pltpu.VMEM),
        ),
        scratch_shapes=scratch,
        compiler_params=pltpu.CompilerParams(
            collective_id=1, has_side_effects=True, vmem_limit_bytes=48 * MIB
        ),
        name="route",
    )(routed, local1, local2, cross1, cross2, grads)


def pool_order(halves):
    rest = halves.shape[2:]
    first = halves[0].reshape((N, N, 2) + rest)
    second = jnp.swapaxes(halves[1].reshape((N, N, 2) + rest), 0, 1)
    return jnp.concatenate([first, second], axis=2).reshape((R,) + rest)


def picks(tables, crossing):
    me = Place()
    grid = tables.reshape(N, N, N, SLOTS)
    coord = jnp.arange(N, dtype=jnp.int32)
    if crossing:
        group, mine = grid[me.x, me.y], me.x * 16 + coord * 4 + me.z + 1
        group = jnp.where(me.core == 1, group[::-1], group)
    else:
        group, mine = grid[:, me.y, me.z], me.x * 16 + me.y * 4 + coord + 1
    sent = jnp.any(tables[None] == mine[:, None, None], axis=2)
    spot = jnp.cumsum(sent.astype(jnp.int32), axis=1) - 1
    spot = jnp.where(sent, spot, -1).astype(jnp.float32).reshape(N, N, N, N)
    if crossing:
        spot = lax.dynamic_index_in_dim(spot, me.y, 2, keepdims=True)
    else:
        spot = lax.dynamic_index_in_dim(spot, me.z, 3, keepdims=True)
        spot = jnp.swapaxes(spot, 1, 2)
    spot = jnp.broadcast_to(spot, (N, N, N, N)).reshape(N, N * N * N)
    return group.astype(jnp.float32).reshape(1, N * SLOTS), spot


def shards(
    activations, cotangents, token_counts, route_ahead, route_back, down_rows, up_rows, norm_gain
):
    sizes = token_counts[0, 0, :SLOTS]
    live = sizes > 0
    entry = [jnp.where(live, to[0, 0, :SLOTS] + 1, 0).astype(jnp.bfloat16) for to in (route_ahead, route_back)]
    table = jnp.concatenate(
        [jnp.pad(row[None], ((i, 15 - i), (0, 128 - SLOTS))) for i, row in enumerate(entry)], axis=0
    )
    own = jnp.stack([down_rows[0, 0], up_rows[0, 0]]).reshape(16, LANE)
    full, tables = gather(own, table)
    full = full.reshape(R, 16, LANE)
    down_full, up_full = full[:, :8].reshape(R, D), full[:, 8:].reshape(R, D)
    section = lax.axis_index("section")
    tables = pool_order(tables[:, :, :2, :SLOTS].astype(jnp.int32))
    from_prev = jnp.where(section > 0, tables[:, 0], 0)
    from_next = jnp.where(section < lax.axis_size("section") - 1, tables[:, 1], 0)

    rows = activations.reshape(-1, D)
    grads = cotangents.reshape(-1, D)
    keep = (jnp.arange(TOK, dtype=jnp.int32)[None, :] < sizes[:, None]).astype(jnp.float32).reshape(ROWS, 1)
    routed, grad_down, grad_up = adapter(rows, grads, keep, down_full, up_full, norm_gain)

    odd = section % 2 == 1
    local, cross = jnp.where(odd, from_prev, from_next), jnp.where(odd, from_next, from_prev)
    local1, local2 = picks(local, False)
    cross1, cross2 = picks(cross, True)
    share = jnp.concatenate([grad_down.reshape(R, 8, LANE), grad_up.reshape(R, 8, LANE)], axis=1)
    ahead, behind, sum_down, sum_up = route(routed, local1, local2, cross1, cross2, share.reshape(R * 16, LANE))
    shape = (1, 1, SLOTS, TOK, D)
    return (ahead.reshape(shape), behind.reshape(shape), sum_down[None], sum_up[None])


def solution(mesh):
    placed = (
        P("section", "pool", None, None, None),
        P("section", "pool", None, None, None),
        P("section", "pool", None),
        P("section", "pool", None),
        P("section", "pool", None),
        P("section", "pool", None),
        P("section", "pool", None),
        P("section", None),
    )
    return jax.shard_map(
        shards,
        mesh=mesh,
        in_specs=placed,
        out_specs=(
            P("section", "pool", None, None, None),
            P("section", "pool", None, None, None),
            P("section", "pool", None),
            P("section", "pool", None),
        ),
        check_vma=False,
    )
```
